32 devices in a mesh: seq: 8 (over y, x, core), fsdp: 4 (over z).
Axes of the slice: x: 2, y: 2, z: 4, core: 2. Of those that a mesh axis runs over, the one named last changes fastest.
Arguments:
- inputs: bfloat16 [8, 2048, 512], P('fsdp', 'seq'), may hold values from -6 to 6
- encoded: bfloat16 [8, 2048, 512], P('fsdp', 'seq'), may hold values from -6 to 6
- cotangent: bfloat16 [8, 2048, 512], P('fsdp', 'seq'), may hold values from -6 to 6
- seg_ids: int32 [8, 2048], P('fsdp'), may hold values from 0 to 15, never falling along the last dimension, each value on 1 to 256 neighbouring positions
- keep_mask: int32 [8, 2048], P('fsdp'), may hold values 0 or 1
- pair_tags: int32 [8, 16], P('fsdp'), may hold values from 0 to 15
- cut_lo: int32 [8, 16], P('fsdp'), may hold values from 0 to 63
- cut_hi: int32 [8, 16], P('fsdp'), may hold values from 0 to 63
- w_query: bfloat16 [512, 512], P('fsdp'), may hold values from -0.25 to 0.25
- w_key: bfloat16 [512, 512], P('fsdp'), may hold values from -0.25 to 0.25
- w_value: bfloat16 [512, 512], P('fsdp'), may hold values from -0.25 to 0.25
- w_out: bfloat16 [512, 512], P('fsdp'), may hold values from -1 to 1
- c_query: bfloat16 [512, 512], P('fsdp'), may hold values from -0.25 to 0.25
- c_key: bfloat16 [512, 512], P('fsdp'), may hold values from -0.25 to 0.25
- c_value: bfloat16 [512, 512], P('fsdp'), may hold values from -0.25 to 0.25
- c_out: bfloat16 [512, 512], P('fsdp'), may hold values from -1 to 1
- w_up: bfloat16 [512, 2048], P('fsdp'), may hold values from -0.25 to 0.25
- w_down: bfloat16 [2048, 512], P('fsdp'), may hold values from -0.25 to 0.25
- gain_one: bfloat16 [512], P('fsdp'), may hold values from 0.5 to 1.5
- bias_one: bfloat16 [512], P('fsdp'), may hold values from -3 to 3
- gain_two: bfloat16 [512], P('fsdp'), may hold values from 0.5 to 1.5
- bias_two: bfloat16 [512], P('fsdp'), may hold values from -3 to 3
- gain_three: bfloat16 [512], P('fsdp'), may hold values from 0.5 to 1.5
- bias_three: bfloat16 [512], P('fsdp'), may hold values from -3 to 3
- tag_table: bfloat16 [16, 512], P(None, 'fsdp'), may hold values from -3 to 3
Outputs:
- output: bfloat16 [8, 2048, 512], P('fsdp', 'seq')
- grad_inputs: bfloat16 [8, 2048, 512], P('fsdp', 'seq')
- grad_encoded: bfloat16 [8, 2048, 512], P('fsdp', 'seq')
- grad_w_query: float32 [512, 512], P('fsdp')
- grad_w_key: float32 [512, 512], P('fsdp')
- grad_w_value: float32 [512, 512], P('fsdp')
- grad_w_out: float32 [512, 512], P('fsdp')
- grad_c_query: float32 [512, 512], P('fsdp')
- grad_c_key: float32 [512, 512], P('fsdp')
- grad_c_value: float32 [512, 512], P('fsdp')
- grad_c_out: float32 [512, 512], P('fsdp')
- grad_w_up: float32 [512, 2048], P('fsdp')
- grad_w_down: float32 [2048, 512], P('fsdp')
- grad_gain_one: float32 [512], P('fsdp')
- grad_bias_one: float32 [512], P('fsdp')
- grad_gain_two: float32 [512], P('fsdp')
- grad_bias_two: float32 [512], P('fsdp')
- grad_gain_three: float32 [512], P('fsdp')
- grad_bias_three: float32 [512], P('fsdp')
- grad_tag_table: float32 [16, 512], P(None, 'fsdp')
The draws below stay inside these ranges and needn't reach their ends.
Inputs may be any that keep to these rules, and one draw needn't show every extreme that they name: `seg_ids`: numbers never fall along a sequence; every number 0 to 15 is used; a sentence has 1 to 256 positions, one exactly 256.
All inputs are finite; a program needn't handle non-finite values. No bound on the sum of `keep_mask` on one device may be relied on, other than what follows from the above.
Results may differ from the reference program's by a relative error of at most 0.028.
Values may be sent and summed in bfloat16 or wider, within the bound.
No kernel may reach another device: no remote copies, remote signals or barrier semaphores. Data moves between devices by JAX's collectives and lax.ppermute only.
A program may use at most 192 MiB of HBM per device.

```python
import math
import jax
import jax.numpy as jnp
import numpy as np
from jax import lax

D = 512
FF = 2048
HEADS = 8
HEAD_DIM = 64
TAGS = 16
MAXLEN = 256
TOK_DEV = 256
LEN = 2048
BATCH = 8
SEGS = 16


def with_ends(entries, stream_key, smallest, top_value):
    longest = entries.shape.index(max(entries.shape))
    spots = []
    for shift in (0, 1):
        where = [jax.random.randint(jax.random.fold_in(stream_key, axis), (), 0, length) for axis, length in enumerate(entries.shape)]
        where[longest] = (where[longest] + shift) % entries.shape[longest]
        spots.append(tuple(where))
    return entries.at[spots[0]].set(smallest).at[spots[1]].set(top_value)


def block_levels(key, dims, shards, least, high):
    gain, own = 1.0, jax.random.fold_in(key, 6)
    for dim, parts in shards:
        heights = jnp.exp(jax.random.uniform(jax.random.fold_in(own, dim), (parts,), jnp.float32, least / len(shards), high / len(shards)))
        gain = gain * jnp.repeat(heights, dims[dim] // parts).reshape([-1 if axis == dim else 1 for axis in range(len(dims))])
    return gain


def profile(amount, total, most, slope):
    loads = [(1 << 20) // math.isqrt(rank ** slope) + 1 for rank in range(2, amount + 1)]
    rest, given = total - most - (amount - 1), [1] * (amount - 1)
    while rest > 0:
        movable = [i for i in range(amount - 1) if given[i] < most]
        pool, left = sum([loads[i] for i in movable]), rest
        for i in movable:
            addition = min(most - given[i], max(1, left * loads[i] // pool), rest)
            given[i] = given[i] + addition
            rest = rest - addition
    return np.array([most] + given)


def ragged_sizes(own_key, count, total, reach, slope):
    if count == 2:
        one = jax.random.randint(own_key, (), max(1, total - reach), min(reach, total - 1) + 1)
        return jnp.stack([one, total - one])
    tallies = jnp.asarray(profile(count, total, reach, slope), jnp.int32)
    pairs = (count - 1) // 2
    source_of, sink = tallies[1:1 + 2 * pairs:2], tallies[2:2 + 2 * pairs:2]
    room = jnp.minimum(source_of - 1, reach - sink)
    shifted = jax.random.randint(jax.random.fold_in(own_key, 1), (pairs,), 0, 1 << 20) % (room + 1)
    tallies = tallies.at[1:1 + 2 * pairs:2].set(source_of - shifted).at[2:2 + 2 * pairs:2].set(sink + shifted)
    return tallies[jax.random.permutation(jax.random.fold_in(own_key, 2), count)]


def bell_draw(rng, extent, deviation, bound, cuts=(), kind=jnp.bfloat16):
    values = jax.random.normal(rng, extent, jnp.float32) * deviation
    if len(cuts) > 0:
        values = block_levels(rng, extent, cuts, -0.22, 0.18) * values
    return jnp.clip(values, min=-bound, max=bound).astype(kind)


def setup_inputs(seed: int = 0) -> dict:
    seeds = jax.random.split(jax.random.key(seed), 26)
    return {
        "inputs": bell_draw(seeds[0], (BATCH, LEN, D), 1.0, 6.0, ((0, 4), (1, 8))),
        "encoded": bell_draw(seeds[1], (BATCH, LEN, D), 1.0, 6.0, ((0, 4), (1, 8))),
        "cotangent": bell_draw(seeds[2], (BATCH, LEN, D), 1.0, 6.0, ((0, 4), (1, 8))),
        "seg_ids": jax.vmap(lambda own: jnp.searchsorted(jnp.cumsum(ragged_sizes(own, SEGS, LEN, MAXLEN, 0)), jnp.arange(LEN), side="right"))(jax.random.split(seeds[3], BATCH)).reshape((BATCH, LEN)).astype(jnp.int32),
        "keep_mask": with_ends((jax.random.randint(seeds[4], (BATCH, LEN), 0, 8) < 7).astype(jnp.int32), jax.random.fold_in(seeds[4], 1), 0, 1),
        "pair_tags": with_ends(jax.random.randint(seeds[5], (BATCH, SEGS), 0, TAGS), jax.random.fold_in(seeds[5], 1), 0, TAGS - 1).astype(jnp.int32),
        "cut_lo": with_ends(jax.random.randint(seeds[6], (BATCH, SEGS), 0, MAXLEN // 4), jax.random.fold_in(seeds[6], 1), 0, (MAXLEN // 4) - 1).astype(jnp.int32),
        "cut_hi": with_ends(jax.random.randint(seeds[7], (BATCH, SEGS), 0, MAXLEN // 4), jax.random.fold_in(seeds[7], 1), 0, (MAXLEN // 4) - 1).astype(jnp.int32),
        "w_query": bell_draw(seeds[8], (D, D), D ** -0.5, 0.25, ((0, 4),)),
        "w_key": bell_draw(seeds[9], (D, D), D ** -0.5, 0.25, ((0, 4),)),
        "w_value": bell_draw(seeds[10], (D, D), D ** -0.5, 0.25, ((0, 4),)),
        "w_out": bell_draw(seeds[11], (D, D), (D // 16) ** -0.5, 1.0, ((0, 4),)),
        "c_query": bell_draw(seeds[12], (D, D), D ** -0.5, 0.25, ((0, 4),)),
        "c_key": bell_draw(seeds[13], (D, D), D ** -0.5, 0.25, ((0, 4),)),
        "c_value": bell_draw(seeds[14], (D, D), D ** -0.5, 0.25, ((0, 4),)),
        "c_out": bell_draw(seeds[15], (D, D), (D // 16) ** -0.5, 1.0, ((0, 4),)),
        "w_up": bell_draw(seeds[16], (D, FF), D ** -0.5, 0.25, ((0, 4),)),
        "w_down": bell_draw(seeds[17], (FF, D), (FF // 4) ** -0.5, 0.25, ((0, 4),)),
        "gain_one": jnp.clip(1.0 + 0.1 * jax.random.normal(seeds[18], (D,), jnp.float32), 0.5, 1.5).astype(jnp.bfloat16),
        "bias_one": bell_draw(seeds[19], (D,), 0.3, 3.0, ((0, 4),)),
        "gain_two": jnp.clip(1.0 + 0.1 * jax.random.normal(seeds[20], (D,), jnp.float32), 0.5, 1.5).astype(jnp.bfloat16),
        "bias_two": bell_draw(seeds[21], (D,), 0.3, 3.0, ((0, 4),)),
        "gain_three": jnp.clip(1.0 + 0.1 * jax.random.normal(seeds[22], (D,), jnp.float32), 0.5, 1.5).astype(jnp.bfloat16),
        "bias_three": bell_draw(seeds[23], (D,), 0.3, 3.0, ((0, 4),)),
        "tag_table": bell_draw(seeds[24], (TAGS, D), 0.5, 3.0, ((1, 4),)),
    }


EPSILON = 1e-05
HIGHEST = lax.Precision.HIGHEST

@jax.custom_vjp
def low(v):
    return lax.optimization_barrier(v.astype(jnp.bfloat16)).astype(jnp.float32)

@jax.custom_vjp
def low_back(v):
    return v

def low_keep(v):
    return (low(v), None)

def low_pass(kept, grad):
    return (grad,)

def back_keep(v):
    return (v, None)

def back_low(kept, grad):
    return (low(grad),)
low.defvjp(low_keep, low_pass)
low_back.defvjp(back_keep, back_low)

def rounded(values_in):
    return low(low_back(values_in))

def matmul(left, right):
    return jnp.dot(left, right, precision=HIGHEST, preferred_element_type=jnp.float32)

def layer_norm(values_in, gain_vec, bias_vec):
    center = values_in - lax.optimization_barrier(jnp.mean(values_in, -1, keepdims=True))
    inverse = lax.rsqrt(lax.optimization_barrier(jnp.mean(center * center, -1, keepdims=True)) + EPSILON)
    return center * inverse * gain_vec + bias_vec

def token_meta(seg_full, cut_lower, cut_upper, pair_row):
    seg_starts = jnp.searchsorted(seg_full, seg_full, side='left').astype(jnp.int32)
    seg_ends = jnp.searchsorted(seg_full, seg_full, side='right').astype(jnp.int32)
    half_len = (seg_ends - seg_starts - 1) // 2
    span_lower = seg_starts + jnp.minimum(cut_lower[seg_full], half_len)
    span_upper = seg_ends - jnp.minimum(cut_upper[seg_full], half_len)
    return (span_lower, span_upper, pair_row[seg_full])

def allowed_mask(query_pos, query_seg, lower_rows, upper_rows, key_pos, key_seg, key_keep, crossing):
    if crossing:
        return (key_pos[None, :] >= lower_rows[:, None]) & (key_pos[None, :] < upper_rows[:, None])
    same_seg = key_seg[None, :] == query_seg[:, None]
    causal = key_pos[None, :] <= query_pos[:, None]
    visible = (key_keep[None, :] == 1) | (key_pos[None, :] == query_pos[:, None])
    return same_seg & causal & visible

def window_attend(queries, keys, values, allowed):
    row_count = queries.shape[0]
    key_count = keys.shape[0]
    heads_q = queries.reshape(row_count, HEADS, HEAD_DIM)
    heads_k = keys.reshape(key_count, HEADS, HEAD_DIM)
    heads_v = values.reshape(key_count, HEADS, HEAD_DIM)
    scores = jnp.einsum('rhd,whd->hrw', heads_q, heads_k, precision=HIGHEST) * HEAD_DIM ** (-0.5)
    scores = low_back(jnp.where(allowed[None], scores, -1e+30))
    highest = lax.optimization_barrier(jnp.max(scores, -1, keepdims=True))
    exponent = jnp.exp(scores - highest)
    weights = low(exponent / lax.optimization_barrier(jnp.sum(exponent, -1, keepdims=True)))
    mixed_out = jnp.einsum('hrw,whd->rhd', weights, heads_v, precision=HIGHEST)
    return mixed_out.reshape(row_count, HEADS * HEAD_DIM)

def attend_sequence(queries, keys, values, row_meta, crossing):
    seg_full, keep_full, span_lower, span_upper = row_meta
    block_rows = min(512, TOK_DEV)
    margin = MAXLEN
    key_span = block_rows + 2 * margin
    key_pad = jnp.pad(keys, ((margin, margin), (0, 0)))
    value_pad = jnp.pad(values, ((margin, margin), (0, 0)))
    seg_pad = jnp.pad(seg_full, margin, constant_values=-1)
    keep_pad = jnp.pad(keep_full, margin)

    def one_block(block_index):
        first_row = block_index * block_rows
        query_blk = lax.dynamic_slice_in_dim(queries, first_row, block_rows, 0)
        key_blk = lax.dynamic_slice_in_dim(key_pad, first_row, key_span, 0)
        value_blk = lax.dynamic_slice_in_dim(value_pad, first_row, key_span, 0)
        query_pos = first_row + jnp.arange(block_rows, dtype=jnp.int32)
        key_pos = first_row - margin + jnp.arange(key_span, dtype=jnp.int32)
        allowed = allowed_mask(query_pos, lax.dynamic_slice_in_dim(seg_full, first_row, block_rows, 0), lax.dynamic_slice_in_dim(span_lower, first_row, block_rows, 0), lax.dynamic_slice_in_dim(span_upper, first_row, block_rows, 0), key_pos, lax.dynamic_slice_in_dim(seg_pad, first_row, key_span, 0), lax.dynamic_slice_in_dim(keep_pad, first_row, key_span, 0), crossing)
        return window_attend(query_blk, key_blk, value_blk, allowed)
    mixed_all = lax.map(jax.checkpoint(one_block), jnp.arange(LEN // block_rows, dtype=jnp.int32))
    return mixed_all.reshape(LEN, D)

def layer(params, inputs, encoded, row_meta, tag_rows):
    w_query, w_key, w_value, w_out, c_query, c_key, c_value, c_out, w_up, w_down, gain_one, bias_one, gain_two, bias_two, gain_three, bias_three, tag_table = params
    tag_hot = (tag_rows[:, None] == jnp.arange(TAGS, dtype=jnp.int32)[None, :]).astype(jnp.float32)
    start = inputs + matmul(tag_hot, tag_table)
    start_low = low(start)
    queries = rounded(matmul(start_low, w_query))
    keys = rounded(matmul(start_low, w_key))
    values = rounded(matmul(start_low, w_value))
    self_mix = rounded(attend_sequence(queries, keys, values, row_meta, False))
    normed_one = layer_norm(start + low_back(matmul(self_mix, w_out)), gain_one, bias_one)
    cross_queries = rounded(matmul(low(normed_one), c_query))
    cross_keys = rounded(matmul(encoded, c_key))
    cross_values = rounded(matmul(encoded, c_value))
    cross_mix = rounded(attend_sequence(cross_queries, cross_keys, cross_values, row_meta, True))
    normed_two = layer_norm(normed_one + low_back(matmul(cross_mix, c_out)), gain_two, bias_two)
    hidden = low_back(matmul(low(normed_two), w_up))
    activated = low(jax.nn.gelu(hidden))
    feed = low_back(matmul(activated, w_down))
    return layer_norm(normed_two + feed, gain_three, bias_three)

def reference(inputs, encoded, cotangent, seg_ids, keep_mask, pair_tags, cut_lo, cut_hi, w_query, w_key, w_value, w_out, c_query, c_key, c_value, c_out, w_up, w_down, gain_one, bias_one, gain_two, bias_two, gain_three, bias_three, tag_table):
    params = tuple((weight.astype(jnp.float32) for weight in (w_query, w_key, w_value, w_out, c_query, c_key, c_value, c_out, w_up, w_down, gain_one, bias_one, gain_two, bias_two, gain_three, bias_three, tag_table)))

    def per_sequence(totals, item):
        seq_in, seq_enc, seq_cot, seg_full, keep_full, pair_row, cut_lower, cut_upper = item
        span_lower, span_upper, tag_rows = token_meta(seg_full, cut_lower, cut_upper, pair_row)
        row_meta = (seg_full, keep_full, span_lower, span_upper)

        def forward(param_set, layer_in, enc_in):
            return layer(param_set, layer_in, enc_in, row_meta, tag_rows)
        result, pullback = jax.vjp(forward, params, seq_in.astype(jnp.float32), seq_enc.astype(jnp.float32))
        grad_params, grad_in, grad_enc = pullback(seq_cot.astype(jnp.float32))
        totals = jax.tree.map(jnp.add, totals, grad_params)
        return (totals, (result.astype(jnp.bfloat16), grad_in.astype(jnp.bfloat16), grad_enc.astype(jnp.bfloat16)))
    zero_grads = jax.tree.map(jnp.zeros_like, params)
    grads, (output, grad_inputs, grad_encoded) = lax.scan(per_sequence, zero_grads, (inputs, encoded, cotangent, seg_ids, keep_mask, pair_tags, cut_lo, cut_hi))
    return (output, grad_inputs, grad_encoded, grads[0], grads[1], grads[2], grads[3], grads[4], grads[5], grads[6], grads[7], grads[8], grads[9], grads[10], grads[11], grads[12], grads[13], grads[14], grads[15], grads[16])
```

```python
import functools

import jax
import jax.numpy as jnp
from jax import lax
from jax.experimental import pallas as pl
from jax.experimental.pallas import tpu as pltpu
from jax.sharding import PartitionSpec as P

HEADS = 8
HEAD_DIM = 64
MAXLEN = 256
LANES = 128
SMALL_ROWS = 32
TAG_ROW = 6
EPSILON = 1e-05
MASKED = -1e30
SCALE = HEAD_DIM ** (-0.5)
BF16 = jnp.bfloat16
F32 = jnp.float32
MIB = 2**20

NN = (((1,), (0,)), ((), ()))
NT = (((1,), (1,)), ((), ()))
TN = (((0,), (0,)), ((), ()))


def dot(left, right, dims=NN):
    return lax.dot_general(left, right, dims, preferred_element_type=F32)


def lane_ids(rows):
    return lax.broadcasted_iota(jnp.int32, (rows, LANES), 1)


def norm_rows(values_in):
    center = values_in - jnp.mean(values_in, -1, keepdims=True)
    inverse = lax.rsqrt(jnp.mean(center * center, -1, keepdims=True) + EPSILON)
    return center * inverse, inverse


def norm_back(grad_rows, unit_rows, inverse, gain):
    scaled = grad_rows * gain
    centered = (
        scaled
        - jnp.mean(scaled, -1, keepdims=True)
        - unit_rows * jnp.mean(scaled * unit_rows, -1, keepdims=True)
    )
    return inverse * centered


def column_sums(values_in):
    return jnp.sum(values_in, 0, keepdims=True)


def attend(queries, keys, values, query_hot, key_bias, own_bias, exps_ref):
    rows, width = queries.shape[0], keys.shape[0]
    low = lane_ids(rows) < HEAD_DIM
    ones = jnp.ones((width, LANES), BF16)
    mixes, inverses = [], []
    for pair in range(HEADS // 2):
        cols = slice(LANES * pair, LANES * (pair + 1))
        pair_q = queries[:, cols]
        pair_k = jnp.concatenate([keys[:, cols], key_bias], 1)
        pair_v = jnp.concatenate([values[:, cols], ones], 1)
        sums = []
        for half in (0, 1):
            mine = low if half == 0 else ~low
            head_q = jnp.concatenate([jnp.where(mine, pair_q, jnp.zeros_like(pair_q)), query_hot], 1)
            scores = dot(head_q, pair_k, NT)
            if own_bias is not None:
                near = width - rows
                scores = jnp.concatenate([scores[:, :near], scores[:, near:] + own_bias], 1)
            highest = jnp.max(scores, -1, keepdims=True)
            exps = jnp.exp(scores - highest).astype(BF16)
            exps_ref[0, 2 * pair + half] = exps
            sums.append(dot(exps, pair_v))
        inverse = 1.0 / jnp.where(low, sums[0][:, LANES:], sums[1][:, LANES:])
        mixes.append(jnp.where(low, sums[0][:, :LANES], sums[1][:, :LANES]) * inverse)
        inverses.append(inverse)
    return jnp.concatenate(mixes, 1), jnp.concatenate(inverses, 1)


def attend_back(queries, keys, values, exps_ref, mix, inverse, grad_mix):
    rows, width = queries.shape[0], keys.shape[0]
    lane = lane_ids(rows)
    low = lane < HEAD_DIM
    low_wide = lane_ids(width) < HEAD_DIM
    two_ones = jnp.where(lane_ids(width) < 2, 1.0, 0.0).astype(BF16)
    grads_q, grads_k, grads_v = [], [], []
    for pair in range(HEADS // 2):
        cols = slice(LANES * pair, LANES * (pair + 1))
        pair_q, pair_k = queries[:, cols], keys[:, cols]
        pair_v = jnp.concatenate([values[:, cols], two_ones], 1)
        scaled = (grad_mix[:, cols].astype(F32) * inverse[:, cols]).astype(BF16)
        product = scaled.astype(F32) * mix[:, cols]
        found_q, found_k, found_v = [], [], []
        for half in (0, 1):
            mine = low if half == 0 else ~low
            centre = jnp.sum(jnp.where(mine, product, 0.0), -1, keepdims=True)
            coarse = centre.astype(BF16).astype(F32)
            shift = jnp.where(lane == 0, -coarse, jnp.where(lane == 1, coarse - centre, 0.0))
            head_g = jnp.concatenate(
                [jnp.where(mine, scaled, jnp.zeros_like(scaled)), shift.astype(BF16)], 1
            )
            exps = exps_ref[0, 2 * pair + half]
            grad_scores = (exps.astype(F32) * dot(head_g, pair_v, NT)).astype(BF16)
            found_q.append(dot(grad_scores, pair_k))
            found_k.append(dot(grad_scores, pair_q, TN))
            found_v.append(dot(exps, scaled, TN))
        grads_q.append(jnp.where(low, found_q[0], found_q[1]) * SCALE)
        grads_k.append(jnp.where(low_wide, found_k[0], found_k[1]))
        grads_v.append(jnp.where(low_wide, found_v[0], found_v[1]))
    return [jnp.concatenate(part, 1).astype(BF16) for part in (grads_q, grads_k, grads_v)]


def matrix(ref, number, width=512):
    return ref[:, number * width : (number + 1) * width]


def self_forward(
    shards,
    before_ref,
    here_ref,
    hot_ref,
    tag_ref,
    bias_ref,
    own_ref,
    weight_ref,
    start_ref,
    low_ref,
    q_ref,
    k_ref,
    v_ref,
    mix_ref,
    inv_ref,
    exps_ref,
    small_ref,
):
    rows = here_ref.shape[1]
    block = 512 // shards
    smalls = jnp.concatenate(
        [
            weight_ref[z * block : z * block + SMALL_ROWS, 1536 : 1536 + block]
            for z in range(shards)
        ],
        1,
    )
    small_ref[...] = smalls.astype(F32)
    seg_tags = dot(tag_ref[0], smalls, TN).astype(BF16)
    hot = hot_ref[0, : MAXLEN + rows]
    tokens = jnp.concatenate([before_ref[0], here_ref[0]], 0).astype(F32)
    start = tokens + dot(hot, seg_tags)
    start_ref[0] = start[MAXLEN:]
    start_low = start.astype(BF16)
    low_ref[0] = start_low
    queries = (dot(start_low[MAXLEN:], matrix(weight_ref, 0)).astype(BF16).astype(F32) * SCALE).astype(BF16)
    keys = dot(start_low, matrix(weight_ref, 1)).astype(BF16)
    values = dot(start_low, matrix(weight_ref, 2)).astype(BF16)
    q_ref[0] = queries
    k_ref[0] = keys
    v_ref[0] = values
    mix_ref[0], inv_ref[0] = attend(
        queries, keys, values, hot[MAXLEN:], bias_ref[0], own_ref[0], exps_ref
    )


def cross_forward(
    start_ref,
    self_mix_ref,
    before_ref,
    here_ref,
    after_ref,
    hot_ref,
    bias_ref,
    small_ref,
    weight_ref,
    norm_low_ref,
    unit_one_ref,
    scale_one_ref,
    q_ref,
    k_ref,
    v_ref,
    mix_ref,
    inv_ref,
    exps_ref,
    normed_ref,
    unit_two_ref,
    scale_two_ref,
):
    rows = start_ref.shape[1]
    source = jnp.concatenate([before_ref[0], here_ref[0], after_ref[0]], 0)
    keys = dot(source, matrix(weight_ref, 2)).astype(BF16)
    values = dot(source, matrix(weight_ref, 3)).astype(BF16)
    k_ref[0] = keys
    v_ref[0] = values
    branch = dot(self_mix_ref[0].astype(BF16), matrix(weight_ref, 0))
    unit_one, scale_one = norm_rows(start_ref[0] + branch)
    unit_one_ref[0] = unit_one
    scale_one_ref[0] = jnp.broadcast_to(scale_one, (rows, LANES))
    normed_one = unit_one * small_ref[0:1] + small_ref[1:2]
    norm_low = normed_one.astype(BF16)
    norm_low_ref[0] = norm_low
    queries = (dot(norm_low, matrix(weight_ref, 1)).astype(BF16).astype(F32) * SCALE).astype(BF16)
    q_ref[0] = queries
    mix, inverse = attend(
        queries, keys, values, hot_ref[0, MAXLEN : MAXLEN + rows], bias_ref[0], None, exps_ref
    )
    mix_ref[0] = mix
    inv_ref[0] = inverse
    branch = dot(mix.astype(BF16), matrix(weight_ref, 4))
    unit_two, scale_two = norm_rows(normed_one + branch)
    unit_two_ref[0] = unit_two
    scale_two_ref[0] = jnp.broadcast_to(scale_two, (rows, LANES))
    normed_ref[0] = unit_two * small_ref[2:3] + small_ref[3:4]


GELU_A = 0.7978845608028654
GELU_B = 0.044715


def feed_both(
    normed_ref,
    unit_ref,
    scale_ref,
    cotangent_ref,
    small_ref,
    weight_ref,
    out_ref,
    back_ref,
    grad_ref,
    sums_ref,
    act_ref,
    slope_ref,
):
    normed = normed_ref[...]
    normed_low = normed.astype(BF16)
    chunks = weight_ref.shape[1] // 1024
    feed = normed
    for part in range(chunks):
        cols = slice(512 * part, 512 * (part + 1))
        hidden = dot(normed_low, matrix(weight_ref, part))
        square = hidden * hidden
        bend = jnp.tanh(hidden * (GELU_A + GELU_A * GELU_B * square))
        rise = 0.5 + 0.5 * bend
        act = (hidden * rise).astype(BF16)
        act_ref[:, cols] = act
        slope_ref[:, cols] = rise + rise * (1.0 - bend) * hidden * (
            GELU_A + 3.0 * GELU_A * GELU_B * square
        )
        feed = feed + dot(act, matrix(weight_ref, chunks + part))
    unit, scale = norm_rows(feed)
    gain = small_ref[4:5]
    out_ref[...] = (unit * gain + small_ref[5:6]).astype(BF16)
    grad = cotangent_ref[...].astype(F32)
    sums_ref[...] = jnp.zeros_like(sums_ref)
    sums_ref[4:5] = column_sums(grad * unit)
    sums_ref[5:6] = column_sums(grad)
    d_three = norm_back(grad, unit, scale, gain)
    d_feed = d_three.astype(BF16)
    total = d_three
    for part in range(chunks):
        cols = slice(512 * part, 512 * (part + 1))
        late = slice(512 * (chunks + part), 512 * (chunks + part + 1))
        grad_ref[:, late] = dot(act_ref[:, cols], d_feed, TN).astype(BF16)
        d_hidden = (
            slope_ref[:, cols] * dot(d_feed, matrix(weight_ref, chunks + part), NT)
        ).astype(BF16)
        grad_ref[:, cols] = dot(normed_low, d_hidden, TN).astype(BF16)
        total = total + dot(d_hidden, matrix(weight_ref, part), NT)
    unit_two = unit_ref[...]
    sums_ref[2:3] = column_sums(total * unit_two)
    sums_ref[3:4] = column_sums(total)
    back_ref[...] = norm_back(total, unit_two, scale_ref[:, 0:1], small_ref[2:3])


def cross_backward(
    back_ref,
    self_mix_ref,
    before_ref,
    here_ref,
    after_ref,
    norm_low_ref,
    unit_ref,
    scale_ref,
    q_ref,
    k_ref,
    v_ref,
    mix_ref,
    inv_ref,
    exps_ref,
    small_ref,
    weight_ref,
    one_ref,
    source_before_ref,
    source_here_ref,
    source_after_ref,
    grad_ref,
    sums_ref,
    total_ref,
):
    step = pl.program_id(0)
    rows = here_ref.shape[1]

    @pl.when(step == 0)
    def _():
        total_ref[...] = jnp.zeros_like(total_ref)
        sums_ref[...] = jnp.zeros_like(sums_ref)

    def add(number, value):
        cols = slice(512 * number, 512 * (number + 1))
        total_ref[:, cols] = total_ref[:, cols] + value

    d_two = back_ref[0]
    d_branch = d_two.astype(BF16)
    mix = mix_ref[0]
    add(4, dot(mix.astype(BF16), d_branch, TN))
    d_mix = dot(d_branch, matrix(weight_ref, 4), NT).astype(BF16)
    d_q, d_k, d_v = attend_back(q_ref[0], k_ref[0], v_ref[0], exps_ref, mix, inv_ref[0], d_mix)
    source = jnp.concatenate([before_ref[0], here_ref[0], after_ref[0]], 0)
    add(2, dot(source, d_k, TN))
    add(3, dot(source, d_v, TN))
    d_source = dot(d_k, matrix(weight_ref, 2), NT) + dot(d_v, matrix(weight_ref, 3), NT)
    source_before_ref[0] = d_source[:MAXLEN].astype(BF16)
    source_here_ref[0] = d_source[MAXLEN : MAXLEN + rows]
    source_after_ref[0] = d_source[MAXLEN + rows :].astype(BF16)
    add(1, dot(norm_low_ref[0], d_q, TN))
    total = d_two + dot(d_q, matrix(weight_ref, 1), NT)
    unit = unit_ref[0]
    sums_ref[0:1] = sums_ref[0:1] + column_sums(total * unit)
    sums_ref[1:2] = sums_ref[1:2] + column_sums(total)
    d_one = norm_back(total, unit, scale_ref[0, :, 0:1], small_ref[0:1])
    one_ref[0] = d_one
    add(0, dot(self_mix_ref[0].astype(BF16), d_one.astype(BF16), TN))

    @pl.when(step == pl.num_programs(0) - 1)
    def _():
        grad_ref[...] = total_ref[...].astype(BF16)


def self_backward(
    shards,
    one_ref,
    low_ref,
    hot_ref,
    tag_ref,
    q_ref,
    k_ref,
    v_ref,
    mix_ref,
    inv_ref,
    exps_ref,
    feed_sums_ref,
    cross_sums_ref,
    out_weight_ref,
    weight_ref,
    before_ref,
    here_ref,
    grad_ref,
    total_ref,
    sums_ref,
):
    step = pl.program_id(0)
    rows = one_ref.shape[1]

    @pl.when(step == 0)
    def _():
        total_ref[...] = jnp.zeros_like(total_ref)
        sums_ref[...] = feed_sums_ref[...] + cross_sums_ref[...]

    def add(number, value):
        cols = slice(512 * number, 512 * (number + 1))
        total_ref[:, cols] = total_ref[:, cols] + value

    d_one = one_ref[0]
    d_mix = dot(d_one.astype(BF16), out_weight_ref[...], NT).astype(BF16)
    d_q, d_k, d_v = attend_back(
        q_ref[0], k_ref[0], v_ref[0], exps_ref, mix_ref[0], inv_ref[0], d_mix
    )
    start_low = low_ref[0]
    add(0, dot(start_low[MAXLEN:], d_q, TN))
    add(1, dot(start_low, d_k, TN))
    add(2, dot(start_low, d_v, TN))
    d_start = dot(d_k, matrix(weight_ref, 1), NT) + dot(d_v, matrix(weight_ref, 2), NT)
    d_before = d_start[:MAXLEN].astype(BF16)
    d_here = d_start[MAXLEN:] + d_one + dot(d_q, matrix(weight_ref, 0), NT)
    before_ref[0] = d_before
    here_ref[0] = d_here
    both = jnp.concatenate([d_before, d_here.astype(BF16)], 0)
    seg_sums = dot(hot_ref[0, : MAXLEN + rows], both, TN)
    coarse = seg_sums.astype(BF16)
    fine = (seg_sums - coarse.astype(F32)).astype(BF16)
    sums_ref[...] = sums_ref[...] + dot(tag_ref[0], coarse) + dot(tag_ref[0], fine)

    @pl.when(step == pl.num_programs(0) - 1)
    def _():
        grad_ref[:, :1536] = total_ref[...].astype(BF16)
        grad_ref[:, 1536:] = jnp.zeros((512, LANES), BF16)
        block = 512 // shards
        for z in range(shards):
            grad_ref[z * block : z * block + SMALL_ROWS, 1536 : 1536 + block] = sums_ref[
                :, z * block : (z + 1) * block
            ].astype(BF16)


def per_step(array):
    rest = (0,) * (array.ndim - 1)
    return pl.BlockSpec((1,) + array.shape[1:], lambda step: (step,) + rest)


def whole(array):
    rest = (0,) * array.ndim
    return pl.BlockSpec(array.shape, lambda step: rest)


def run_steps(body, name, stepped, fixed, stepped_outs, fixed_outs, scratch=(), order=None):
    batch = stepped[0].shape[0]
    outs = [jax.ShapeDtypeStruct(*spec) for spec in (*stepped_outs, *fixed_outs)]
    count = len(stepped_outs)
    return pl.pallas_call(
        body,
        grid=(batch,),
        in_specs=[per_step(a) for a in stepped] + [whole(a) for a in fixed],
        out_specs=[per_step(a) for a in outs[:count]] + [whole(a) for a in outs[count:]],
        out_shape=outs,
        scratch_shapes=list(scratch),
        compiler_params=pltpu.CompilerParams(vmem_limit_bytes=48 * MIB),
        name=name,
    )(*stepped, *fixed)


def gather_weights(*packs):
    return [lax.all_gather(pack, "fsdp", axis=0, tiled=True) for pack in packs]


def reduce_grads(*grads):
    return [
        lax.psum(lax.psum_scatter(grad, "fsdp", scatter_dimension=0, tiled=True), "seq")
        for grad in grads
    ]


def local_facts(seg_ids, keep_mask, pair_tags, cut_lo, cut_hi, base, rows):
    sentences = pair_tags.shape[1]
    ids = jnp.arange(sentences, dtype=jnp.int32)
    starts = jnp.sum(seg_ids[:, :, None] < ids, 1, dtype=jnp.int32)
    ends = jnp.sum(seg_ids[:, :, None] <= ids, 1, dtype=jnp.int32)
    half = (ends - starts - 1) // 2
    spare = ((0, 0), (0, LANES - sentences))
    lower = jnp.pad(starts + jnp.minimum(cut_lo, half), spare)
    upper = jnp.pad(ends - jnp.minimum(cut_hi, half), spare)
    edge = ((0, 0), (MAXLEN, MAXLEN))
    width = rows + 2 * MAXLEN
    seg = lax.dynamic_slice_in_dim(jnp.pad(seg_ids, edge, constant_values=-1), base, width, 1)
    keep = lax.dynamic_slice_in_dim(jnp.pad(keep_mask, edge), base, width, 1)
    lanes = jnp.arange(LANES, dtype=jnp.int32)
    hot = seg[:, :, None] == lanes
    place = base - MAXLEN + jnp.arange(width, dtype=jnp.int32)[None, :, None]
    inside = (place >= lower[:, None, :]) & (place < upper[:, None, :])
    near = MAXLEN + rows
    seen = (keep[:, :near] == 1) | (jnp.arange(near) >= MAXLEN)
    self_bias = jnp.where(hot[:, :near] & seen[:, :, None], 0.0, MASKED).astype(BF16)
    cross_bias = jnp.where(inside, 0.0, MASKED).astype(BF16)
    spot = jnp.arange(rows, dtype=jnp.int32)
    earlier = (spot[None, :] < spot[:, None]) & (keep[:, None, MAXLEN:near] == 1)
    own_bias = jnp.where(earlier | (spot[None, :] == spot[:, None]), 0.0, MASKED).astype(F32)
    tag_rows = TAG_ROW + pair_tags
    tags = (tag_rows[:, None, :] == jnp.arange(SMALL_ROWS, dtype=jnp.int32)[:, None]).astype(BF16)
    tags = jnp.pad(tags, ((0, 0), (0, 0), (0, LANES - sentences)))
    return hot.astype(BF16), self_bias, cross_bias, own_bias, tags


def shifted(shard, by):
    size = lax.axis_size("seq")
    pairs = [(i, i + by) for i in range(size) if 0 <= i + by < size]
    return lax.ppermute(shard, "seq", pairs)


def on_device(
    inputs,
    encoded,
    cotangent,
    seg_ids,
    keep_mask,
    pair_tags,
    cut_lo,
    cut_hi,
    w_query,
    w_key,
    w_value,
    w_out,
    c_query,
    c_key,
    c_value,
    c_out,
    w_up,
    w_down,
    gain_one,
    bias_one,
    gain_two,
    bias_two,
    gain_three,
    bias_three,
    tag_table,
):
    batch, rows, _ = inputs.shape
    shards = lax.axis_size("fsdp")
    block = w_query.shape[0]
    chunks = w_down.shape[0] // block
    base = lax.axis_index("seq") * rows
    small = jnp.concatenate(
        [
            jnp.stack([gain_one, bias_one, gain_two, bias_two, gain_three, bias_three]),
            tag_table,
        ],
        0,
    )
    small = jnp.pad(small, ((0, block - small.shape[0]), (0, LANES - small.shape[1])))
    up = w_up.reshape(block, shards, chunks, block).swapaxes(1, 2).reshape(block, -1)
    down = w_down.reshape(chunks, block, 512).swapaxes(0, 1).reshape(block, -1)
    pack_one = jnp.concatenate([w_query, w_key, w_value, small], 1)
    pack_two = jnp.concatenate([w_out, c_query, c_key, c_value, c_out], 1)
    pack_three = jnp.concatenate([up, down], 1)
    full_one, full_two, full_three = gather_weights(pack_one, pack_two, pack_three)

    inputs_before = shifted(inputs, 1)
    encoded_before = shifted(encoded, 1)
    encoded_after = shifted(encoded, -1)
    hot, self_bias, cross_bias, own_bias, tags = local_facts(
        seg_ids, keep_mask, pair_tags, cut_lo, cut_hi, base, rows
    )
    near, wide = MAXLEN + rows, 2 * MAXLEN + rows

    def tokens(count, kind, width=512):
        return ((batch, count, width), kind)

    start, start_low, s_q, s_k, s_v, s_mix, s_inv, s_exps, smalls = run_steps(
        functools.partial(self_forward, shards),
        "self_forward",
        (inputs_before, inputs, hot, tags, self_bias, own_bias),
        (full_one,),
        (
            tokens(rows, F32),
            tokens(near, BF16),
            tokens(rows, BF16),
            tokens(near, BF16),
            tokens(near, BF16),
            tokens(rows, F32),
            tokens(rows, F32),
            ((batch, HEADS, rows, near), BF16),
        ),
        (((SMALL_ROWS, 512), F32),),
    )
    (
        norm_low,
        unit_one,
        scale_one,
        c_q,
        c_k,
        c_v,
        c_mix,
        c_inv,
        c_exps,
        normed_two,
        unit_two,
        scale_two,
    ) = run_steps(
        cross_forward,
        "cross_forward",
        (start, s_mix, encoded_before, encoded, encoded_after, hot, cross_bias),
        (smalls, full_two),
        (
            tokens(rows, BF16),
            tokens(rows, F32),
            tokens(rows, F32, LANES),
            tokens(rows, BF16),
            tokens(wide, BF16),
            tokens(wide, BF16),
            tokens(rows, F32),
            tokens(rows, F32),
            ((batch, HEADS, rows, wide), BF16),
            tokens(rows, F32),
            tokens(rows, F32),
            tokens(rows, F32, LANES),
        ),
        (),
    )
    count = batch * rows
    hidden = 512 * chunks

    def flat(array):
        return array.reshape(count, array.shape[-1])

    output, d_two, grad_three, feed_sums = pl.pallas_call(
        feed_both,
        out_shape=[
            jax.ShapeDtypeStruct((count, 512), BF16),
            jax.ShapeDtypeStruct((count, 512), F32),
            jax.ShapeDtypeStruct((512, 2 * hidden), BF16),
            jax.ShapeDtypeStruct((SMALL_ROWS, 512), F32),
        ],
        scratch_shapes=[pltpu.VMEM((count, hidden), BF16), pltpu.VMEM((count, hidden), F32)],
        compiler_params=pltpu.CompilerParams(vmem_limit_bytes=48 * MIB),
        name="feed_both",
    )(flat(normed_two), flat(unit_two), flat(scale_two), flat(cotangent), smalls, full_three)
    d_one, source_before, source_here, source_after, grad_two, cross_sums = run_steps(
        cross_backward,
        "cross_backward",
        (
            d_two.reshape(batch, rows, 512),
            s_mix,
            encoded_before,
            encoded,
            encoded_after,
            norm_low,
            unit_one,
            scale_one,
            c_q,
            c_k,
            c_v,
            c_mix,
            c_inv,
            c_exps,
        ),
        (smalls, full_two),
        (
            tokens(rows, F32),
            tokens(MAXLEN, BF16),
            tokens(rows, F32),
            tokens(MAXLEN, BF16),
        ),
        (((512, 2560), BF16), ((SMALL_ROWS, 512), F32)),
        (pltpu.VMEM((512, 2560), F32),),
    )
    grad_encoded = (source_here + shifted(source_before, -1) + shifted(source_after, 1)).astype(BF16)
    start_before, start_here, grad_one = run_steps(
        functools.partial(self_backward, shards),
        "self_backward",
        (d_one, start_low, hot, tags, s_q, s_k, s_v, s_mix, s_inv, s_exps),
        (feed_sums, cross_sums, full_two[:, :512], full_one),
        (tokens(MAXLEN, BF16), tokens(rows, F32)),
        (((512, 1536 + LANES), BF16),),
        (pltpu.VMEM((512, 1536), F32), pltpu.VMEM((SMALL_ROWS, 512), F32)),
    )
    grad_inputs = (start_here + shifted(start_before, -1)).astype(BF16)
    grad_one, grad_two, grad_three = reduce_grads(grad_one, grad_two, grad_three)

    def part(array, number):
        return array[:, 512 * number : 512 * (number + 1)].astype(F32)

    small_sums = grad_one[:, 1536:].astype(F32)
    grad_up = grad_three[:, :hidden].reshape(block, chunks, shards, block).swapaxes(1, 2)
    grad_down = grad_three[:, hidden:].reshape(block, chunks, 512).swapaxes(0, 1)
    return (
        output.reshape(batch, rows, 512),
        grad_inputs,
        grad_encoded,
        part(grad_one, 0),
        part(grad_one, 1),
        part(grad_one, 2),
        part(grad_two, 0),
        part(grad_two, 1),
        part(grad_two, 2),
        part(grad_two, 3),
        part(grad_two, 4),
        grad_up.reshape(block, hidden).astype(F32),
        grad_down.reshape(chunks * block, 512).astype(F32),
        *(small_sums[row, :block] for row in range(TAG_ROW)),
        small_sums[TAG_ROW : TAG_ROW + tag_table.shape[0], :block],
    )


def solution(mesh):
    rows = P("fsdp", "seq", None)
    by_row = P("fsdp", None)
    vector = P("fsdp")
    tags = P(None, "fsdp")
    return jax.shard_map(
        on_device,
        mesh=mesh,
        in_specs=(rows,) * 3 + (by_row,) * 15 + (vector,) * 6 + (tags,),
        out_specs=(rows,) * 3 + (by_row,) * 10 + (vector,) * 6 + (tags,),
        check_vma=False,
    )
```

```python
import functools

import jax
import jax.numpy as jnp
from jax import lax
from jax.experimental import pallas as pl
from jax.experimental.pallas import tpu as pltpu
from jax.sharding import PartitionSpec as P

HEADS = 8
HEAD_DIM = 64
MAXLEN = 256
LANES = 128
SMALL_ROWS = 32
TAG_ROW = 6
EPSILON = 1e-05
MASKED = -1e30
SCALE = HEAD_DIM ** (-0.5)
BF16 = jnp.bfloat16
F32 = jnp.float32
MIB = 2**20
PER_US = 10**9

NN = (((1,), (0,)), ((), ()))
NT = (((1,), (1,)), ((), ()))
TN = (((0,), (0,)), ((), ()))


def dot(left, right, dims=NN):
    return lax.dot_general(left, right, dims, preferred_element_type=F32)


def lane_ids(rows):
    return lax.broadcasted_iota(jnp.int32, (rows, LANES), 1)


def norm_rows(values_in):
    center = values_in - jnp.mean(values_in, -1, keepdims=True)
    inverse = lax.rsqrt(jnp.mean(center * center, -1, keepdims=True) + EPSILON)
    return center * inverse, inverse


def norm_back(grad_rows, unit_rows, inverse, gain):
    scaled = grad_rows * gain
    centered = (
        scaled
        - jnp.mean(scaled, -1, keepdims=True)
        - unit_rows * jnp.mean(scaled * unit_rows, -1, keepdims=True)
    )
    return inverse * centered


def column_sums(values_in):
    return jnp.sum(values_in, 0, keepdims=True)


def attend(queries, keys, values, query_hot, key_bias, own_bias, exps_ref):
    rows, width = queries.shape[0], keys.shape[0]
    low = lane_ids(rows) < HEAD_DIM
    ones = jnp.ones((width, LANES), BF16)
    mixes, inverses = [], []
    for pair in range(HEADS // 2):
        cols = slice(LANES * pair, LANES * (pair + 1))
        pair_q = queries[:, cols]
        pair_k = jnp.concatenate([keys[:, cols], key_bias], 1)
        pair_v = jnp.concatenate([values[:, cols], ones], 1)
        sums = []
        for half in (0, 1):
            mine = low if half == 0 else ~low
            head_q = jnp.concatenate([jnp.where(mine, pair_q, jnp.zeros_like(pair_q)), query_hot], 1)
            scores = dot(head_q, pair_k, NT)
            if own_bias is not None:
                near = width - rows
                scores = jnp.concatenate([scores[:, :near], scores[:, near:] + own_bias], 1)
            highest = jnp.max(scores, -1, keepdims=True)
            exps = jnp.exp(scores - highest).astype(BF16)
            exps_ref[0, 2 * pair + half] = exps
            sums.append(dot(exps, pair_v))
        inverse = 1.0 / jnp.where(low, sums[0][:, LANES:], sums[1][:, LANES:])
        mixes.append(jnp.where(low, sums[0][:, :LANES], sums[1][:, :LANES]) * inverse)
        inverses.append(inverse)
    return jnp.concatenate(mixes, 1), jnp.concatenate(inverses, 1)


def attend_back(queries, keys, values, exps_ref, mix, inverse, grad_mix):
    rows, width = queries.shape[0], keys.shape[0]
    lane = lane_ids(rows)
    low = lane < HEAD_DIM
    low_wide = lane_ids(width) < HEAD_DIM
    two_ones = jnp.where(lane_ids(width) < 2, 1.0, 0.0).astype(BF16)
    grads_q, grads_k, grads_v = [], [], []
    for pair in range(HEADS // 2):
        cols = slice(LANES * pair, LANES * (pair + 1))
        pair_q, pair_k = queries[:, cols], keys[:, cols]
        pair_v = jnp.concatenate([values[:, cols], two_ones], 1)
        scaled = (grad_mix[:, cols].astype(F32) * inverse[:, cols]).astype(BF16)
        product = scaled.astype(F32) * mix[:, cols]
        found_q, found_k, found_v = [], [], []
        for half in (0, 1):
            mine = low if half == 0 else ~low
            centre = jnp.sum(jnp.where(mine, product, 0.0), -1, keepdims=True)
            coarse = centre.astype(BF16).astype(F32)
            shift = jnp.where(lane == 0, -coarse, jnp.where(lane == 1, coarse - centre, 0.0))
            head_g = jnp.concatenate(
                [jnp.where(mine, scaled, jnp.zeros_like(scaled)), shift.astype(BF16)], 1
            )
            exps = exps_ref[0, 2 * pair + half]
            grad_scores = (exps.astype(F32) * dot(head_g, pair_v, NT)).astype(BF16)
            found_q.append(dot(grad_scores, pair_k))
            found_k.append(dot(grad_scores, pair_q, TN))
            found_v.append(dot(exps, scaled, TN))
        grads_q.append(jnp.where(low, found_q[0], found_q[1]) * SCALE)
        grads_k.append(jnp.where(low_wide, found_k[0], found_k[1]))
        grads_v.append(jnp.where(low_wide, found_v[0], found_v[1]))
    return [jnp.concatenate(part, 1).astype(BF16) for part in (grads_q, grads_k, grads_v)]


def matrix(ref, number, width=512):
    return ref[:, number * width : (number + 1) * width]


def self_forward(
    shards,
    where_ref,
    before_ref,
    here_ref,
    hot_ref,
    tag_ref,
    bias_ref,
    own_ref,
    weight_ref,
    start_ref,
    low_ref,
    q_ref,
    k_ref,
    v_ref,
    mix_ref,
    inv_ref,
    exps_ref,
    small_ref,
):
    rows = here_ref.shape[1]
    block = 512 // shards
    smalls = jnp.concatenate(
        [
            weight_ref[z * block : z * block + SMALL_ROWS, 1536 : 1536 + block]
            for z in range(shards)
        ],
        1,
    )
    small_ref[...] = smalls.astype(F32)
    seg_tags = dot(tag_ref[0], smalls, TN).astype(BF16)
    hot = hot_ref[0, : MAXLEN + rows]
    tokens = jnp.concatenate([before_ref[0], here_ref[0]], 0).astype(F32)
    start = tokens + dot(hot, seg_tags)
    start_ref[0] = start[MAXLEN:]
    start_low = start.astype(BF16)
    low_ref[0] = start_low
    queries = (dot(start_low[MAXLEN:], matrix(weight_ref, 0)).astype(BF16).astype(F32) * SCALE).astype(BF16)
    keys = dot(start_low, matrix(weight_ref, 1)).astype(BF16)
    values = dot(start_low, matrix(weight_ref, 2)).astype(BF16)
    q_ref[0] = queries
    k_ref[0] = keys
    v_ref[0] = values
    mix_ref[0], inv_ref[0] = attend(
        queries, keys, values, hot[MAXLEN:], bias_ref[0], own_ref[0], exps_ref
    )


def cross_forward(
    where_ref,
    start_ref,
    self_mix_ref,
    before_ref,
    here_ref,
    after_ref,
    hot_ref,
    bias_ref,
    small_ref,
    weight_ref,
    norm_low_ref,
    unit_one_ref,
    scale_one_ref,
    q_ref,
    k_ref,
    v_ref,
    mix_ref,
    inv_ref,
    exps_ref,
    normed_ref,
    unit_two_ref,
    scale_two_ref,
):
    rows = start_ref.shape[1]
    source = jnp.concatenate([before_ref[0], here_ref[0], after_ref[0]], 0)
    keys = dot(source, matrix(weight_ref, 2)).astype(BF16)
    values = dot(source, matrix(weight_ref, 3)).astype(BF16)
    k_ref[0] = keys
    v_ref[0] = values
    branch = dot(self_mix_ref[0].astype(BF16), matrix(weight_ref, 0))
    unit_one, scale_one = norm_rows(start_ref[0] + branch)
    unit_one_ref[0] = unit_one
    scale_one_ref[0] = jnp.broadcast_to(scale_one, (rows, LANES))
    normed_one = unit_one * small_ref[0:1] + small_ref[1:2]
    norm_low = normed_one.astype(BF16)
    norm_low_ref[0] = norm_low
    queries = (dot(norm_low, matrix(weight_ref, 1)).astype(BF16).astype(F32) * SCALE).astype(BF16)
    q_ref[0] = queries
    mix, inverse = attend(
        queries, keys, values, hot_ref[0, MAXLEN : MAXLEN + rows], bias_ref[0], None, exps_ref
    )
    mix_ref[0] = mix
    inv_ref[0] = inverse
    branch = dot(mix.astype(BF16), matrix(weight_ref, 4))
    unit_two, scale_two = norm_rows(normed_one + branch)
    unit_two_ref[0] = unit_two
    scale_two_ref[0] = jnp.broadcast_to(scale_two, (rows, LANES))
    normed_ref[0] = unit_two * small_ref[2:3] + small_ref[3:4]


GELU_A = 0.7978845608028654
GELU_B = 0.044715


def feed_both(
    shards,
    pieces,
    grads,
    where_ref,
    normed_ref,
    unit_ref,
    scale_ref,
    cotangent_ref,
    small_ref,
    *rest,
):
    piece_refs, rest = rest[:pieces], rest[pieces:]
    out_ref, back_ref, sums_ref, *rest = rest
    grad_refs, rest = rest[:grads], rest[grads:]
    act_ref, slope_ref, grad_ref, *rest = rest
    weight_ref = piece_refs[0]
    if pieces > 1:
        (weight_ref,) = rest
        assemble(where_ref, piece_refs, weight_ref)
    normed = normed_ref[...]
    normed_low = normed.astype(BF16)
    chunks = weight_ref.shape[1] // 1024
    feed = normed
    for part in range(chunks):
        cols = slice(512 * part, 512 * (part + 1))
        hidden = dot(normed_low, matrix(weight_ref, part))
        square = hidden * hidden
        bend = jnp.tanh(hidden * (GELU_A + GELU_A * GELU_B * square))
        rise = 0.5 + 0.5 * bend
        act = (hidden * rise).astype(BF16)
        act_ref[:, cols] = act
        slope_ref[:, cols] = rise + rise * (1.0 - bend) * hidden * (
            GELU_A + 3.0 * GELU_A * GELU_B * square
        )
        feed = feed + dot(act, matrix(weight_ref, chunks + part))
    unit, scale = norm_rows(feed)
    gain = small_ref[4:5]
    out_ref[...] = (unit * gain + small_ref[5:6]).astype(BF16)
    grad = cotangent_ref[...].astype(F32)
    sums_ref[...] = jnp.zeros_like(sums_ref)
    sums_ref[4:5] = column_sums(grad * unit)
    sums_ref[5:6] = column_sums(grad)
    d_three = norm_back(grad, unit, scale, gain)
    d_feed = d_three.astype(BF16)
    total = d_three
    for part in range(chunks):
        cols = slice(512 * part, 512 * (part + 1))
        late = slice(512 * (chunks + part), 512 * (chunks + part + 1))
        grad_ref[:, late] = dot(act_ref[:, cols], d_feed, TN).astype(BF16)
        d_hidden = (
            slope_ref[:, cols] * dot(d_feed, matrix(weight_ref, chunks + part), NT)
        ).astype(BF16)
        grad_ref[:, cols] = dot(normed_low, d_hidden, TN).astype(BF16)
        total = total + dot(d_hidden, matrix(weight_ref, part), NT)
    unit_two = unit_ref[...]
    sums_ref[2:3] = column_sums(total * unit_two)
    sums_ref[3:4] = column_sums(total)
    back_ref[...] = norm_back(total, unit_two, scale_ref[:, 0:1], small_ref[2:3])
    give(shards, where_ref, grad_ref, grad_refs)


def cross_backward(
    shards,
    where_ref,
    back_ref,
    self_mix_ref,
    before_ref,
    here_ref,
    after_ref,
    norm_low_ref,
    unit_ref,
    scale_ref,
    q_ref,
    k_ref,
    v_ref,
    mix_ref,
    inv_ref,
    exps_ref,
    small_ref,
    weight_ref,
    one_ref,
    d_mix_ref,
    source_before_ref,
    source_here_ref,
    source_after_ref,
    sums_ref,
    *rest,
):
    *grad_refs, total_ref = rest
    step = pl.program_id(0)
    rows = here_ref.shape[1]

    @pl.when(step == 0)
    def _():
        total_ref[...] = jnp.zeros_like(total_ref)
        sums_ref[...] = jnp.zeros_like(sums_ref)

    def add(number, value):
        cols = slice(512 * number, 512 * (number + 1))
        total_ref[:, cols] = total_ref[:, cols] + value

    d_two = back_ref[0]
    d_branch = d_two.astype(BF16)
    mix = mix_ref[0]
    add(4, dot(mix.astype(BF16), d_branch, TN))
    d_mix = dot(d_branch, matrix(weight_ref, 4), NT).astype(BF16)
    d_q, d_k, d_v = attend_back(q_ref[0], k_ref[0], v_ref[0], exps_ref, mix, inv_ref[0], d_mix)
    source = jnp.concatenate([before_ref[0], here_ref[0], after_ref[0]], 0)
    add(2, dot(source, d_k, TN))
    add(3, dot(source, d_v, TN))
    d_source = dot(d_k, matrix(weight_ref, 2), NT) + dot(d_v, matrix(weight_ref, 3), NT)
    source_before_ref[0] = d_source[:MAXLEN].astype(BF16)
    source_here_ref[0] = d_source[MAXLEN : MAXLEN + rows]
    source_after_ref[0] = d_source[MAXLEN + rows :].astype(BF16)
    add(1, dot(norm_low_ref[0], d_q, TN))
    total = d_two + dot(d_q, matrix(weight_ref, 1), NT)
    unit = unit_ref[0]
    sums_ref[0:1] = sums_ref[0:1] + column_sums(total * unit)
    sums_ref[1:2] = sums_ref[1:2] + column_sums(total)
    d_one = norm_back(total, unit, scale_ref[0, :, 0:1], small_ref[0:1])
    one_ref[0] = d_one
    d_one_low = d_one.astype(BF16)
    add(0, dot(self_mix_ref[0].astype(BF16), d_one_low, TN))
    d_mix_ref[0] = dot(d_one_low, matrix(weight_ref, 0), NT).astype(BF16)

    @pl.when(step == pl.num_programs(0) - 1)
    def _():
        give(shards, where_ref, total_ref, grad_refs)


def self_backward(
    shards,
    where_ref,
    one_ref,
    d_mix_ref,
    low_ref,
    hot_ref,
    tag_ref,
    q_ref,
    k_ref,
    v_ref,
    mix_ref,
    inv_ref,
    exps_ref,
    feed_sums_ref,
    cross_sums_ref,
    weight_ref,
    before_ref,
    here_ref,
    *rest,
):
    *grad_refs, total_ref, sums_ref = rest
    step = pl.program_id(0)
    rows = one_ref.shape[1]

    @pl.when(step == 0)
    def _():
        total_ref[...] = jnp.zeros_like(total_ref)
        sums_ref[...] = feed_sums_ref[...] + cross_sums_ref[...]

    def add(number, value):
        cols = slice(512 * number, 512 * (number + 1))
        total_ref[:, cols] = total_ref[:, cols] + value

    d_one = one_ref[0]
    d_mix = d_mix_ref[0]
    d_q, d_k, d_v = attend_back(
        q_ref[0], k_ref[0], v_ref[0], exps_ref, mix_ref[0], inv_ref[0], d_mix
    )
    start_low = low_ref[0]
    add(0, dot(start_low[MAXLEN:], d_q, TN))
    add(1, dot(start_low, d_k, TN))
    add(2, dot(start_low, d_v, TN))
    d_start = dot(d_k, matrix(weight_ref, 1), NT) + dot(d_v, matrix(weight_ref, 2), NT)
    d_before = d_start[:MAXLEN].astype(BF16)
    d_here = d_start[MAXLEN:] + d_one + dot(d_q, matrix(weight_ref, 0), NT)
    before_ref[0] = d_before
    here_ref[0] = d_here
    both = jnp.concatenate([d_before, d_here.astype(BF16)], 0)
    seg_sums = dot(hot_ref[0, : MAXLEN + rows], both, TN)
    coarse = seg_sums.astype(BF16)
    fine = (seg_sums - coarse.astype(F32)).astype(BF16)
    sums_ref[...] = sums_ref[...] + dot(tag_ref[0], coarse) + dot(tag_ref[0], fine)

    @pl.when(step == pl.num_programs(0) - 1)
    def _():
        block = 512 // shards
        for z in range(shards):
            total_ref[z * block : z * block + SMALL_ROWS, 1536 : 1536 + block] = sums_ref[
                :, z * block : (z + 1) * block
            ]
        give(shards, where_ref, total_ref, grad_refs)


def busy(micros):
    return pl.CostEstimate(
        flops=micros * PER_US, bytes_accessed=micros * 2 * MIB, transcendentals=0
    )


def per_step(array):
    rest = (0,) * (array.ndim - 1)
    return pl.BlockSpec((1,) + array.shape[1:], lambda step: (step,) + rest)


def whole(array):
    rest = (0,) * array.ndim
    return pl.BlockSpec(array.shape, lambda step: rest)


def run_steps(
    body, name, micros, where, stepped, fixed, weights, stepped_outs, fixed_outs, scratch=()
):
    batch = stepped[0].shape[0]
    outs = [jax.ShapeDtypeStruct(*spec) for spec in (*stepped_outs, *fixed_outs)]
    counts = [len(stepped), len(fixed), *(len(pieces) for pieces in weights)]
    outs_count = len(outs)
    whole_scratch = [
        pltpu.VMEM((512, pieces[0].shape[-1]), BF16) for pieces in weights if len(pieces) > 1
    ]

    def called(where_ref, *refs):
        refs = list(refs)

        def take(count):
            taken = refs[:count]
            del refs[:count]
            return taken

        plain = take(counts[0] + counts[1])
        pieces = [take(count) for count in counts[2:]]
        outs_refs = take(outs_count)
        own_scratch = take(len(scratch))
        fulls = []
        for piece_refs in pieces:
            if len(piece_refs) == 1:
                fulls.append(piece_refs[0])
                continue
            (full_ref,) = take(1)
            fulls.append(full_ref)

            @pl.when(pl.program_id(0) == 0)
            def _(piece_refs=piece_refs, full_ref=full_ref):
                assemble(where_ref, piece_refs, full_ref)

        body(where_ref, *plain, *fulls, *outs_refs, *own_scratch)

    flat_weights = [piece for pieces in weights for piece in pieces]
    steps = len(stepped_outs)
    return pl.pallas_call(
        called,
        grid=(batch,),
        in_specs=[pl.BlockSpec(memory_space=pltpu.SMEM)]
        + [per_step(a) for a in stepped]
        + [whole(a) for a in (*fixed, *flat_weights)],
        out_specs=[per_step(a) for a in outs[:steps]] + [whole(a) for a in outs[steps:]],
        out_shape=outs,
        scratch_shapes=[*scratch, *whole_scratch],
        compiler_params=pltpu.CompilerParams(vmem_limit_bytes=48 * MIB),
        cost_estimate=busy(micros),
        name=name,
    )(where, *stepped, *fixed, *flat_weights)


def grad_specs(block, columns):
    if not by_shares(block):
        return (((512, columns), BF16),)
    places = lax.axis_size("seq")
    return (((places // 2, 512 // places, columns), BF16),) * 2


def give(shards, where_ref, total_ref, refs):
    if len(refs) == 1:
        refs[0][...] = total_ref[...].astype(BF16)
    else:
        split_shares(shards, where_ref, total_ref, *refs)


def pack_body(chunks, shards, place_ref, *refs):
    ins, (low_ref, mid_ref, late_ref, small_ref) = refs[:-4], refs[-4:]
    squares, (up_ref, down_ref, tag_ref), vectors = ins[:8], ins[8:11], ins[11:]
    eighth, fourth = low_ref.shape[0], late_ref.shape[0]
    block = small_ref.shape[0]
    small_ref[...] = jnp.zeros_like(small_ref)
    for row, vector_ref in enumerate(vectors):
        small_ref[row : row + 1, :block] = vector_ref[...].astype(F32)
    small_ref[TAG_ROW : TAG_ROW + tag_ref.shape[0], :block] = tag_ref[...].astype(F32)
    for number in range(3):
        low_ref[:, 512 * number : 512 * (number + 1)] = squares[number][...]
    row = pl.multiple_of(place_ref[0] * eighth, eighth)
    low_ref[:, 1536:] = small_ref[pl.ds(row, eighth), :].astype(BF16)
    for number in range(5):
        mid_ref[:, 512 * number : 512 * (number + 1)] = squares[3 + number][...]
    for part in range(chunks):
        for shard in range(shards):
            here = (shard * chunks + part) * block
            there = part * 512 + shard * block
            late_ref[:, there : there + block] = up_ref[:, here : here + block]
        lane = 512 * (chunks + part)
        late_ref[:, lane : lane + 512] = down_ref[part]


def pack_shares(places, chunks, shards, squares, up, down, tags, vectors):
    block = squares[0].shape[0]
    eighth, fourth = block // 8, block // 4

    def rows_at(number):
        return lambda step, place: (place[number], 0)

    return pl.pallas_call(
        functools.partial(pack_body, chunks, shards),
        grid_spec=pltpu.PrefetchScalarGridSpec(
            num_scalar_prefetch=1,
            grid=(1,),
            in_specs=[pl.BlockSpec((eighth, 512), rows_at(0))] * 8
            + [
                pl.BlockSpec((fourth, up.shape[1]), rows_at(1)),
                pl.BlockSpec((chunks, fourth, 512), lambda step, place: (0, place[2], 0)),
                pl.BlockSpec(tags.shape, lambda step, place: (0, 0)),
            ]
            + [pl.BlockSpec((1, block), lambda step, place: (0, 0))] * len(vectors),
            out_specs=[
                pl.BlockSpec((eighth, 1536 + LANES), lambda step, place: (0, 0)),
                pl.BlockSpec((eighth, 2560), lambda step, place: (0, 0)),
                pl.BlockSpec((fourth, 2 * up.shape[1]), lambda step, place: (0, 0)),
            ],
            scratch_shapes=[pltpu.VMEM((block, LANES), F32)],
        ),
        out_shape=[
            jax.ShapeDtypeStruct((eighth, 1536 + LANES), BF16),
            jax.ShapeDtypeStruct((eighth, 2560), BF16),
            jax.ShapeDtypeStruct((fourth, 2 * up.shape[1]), BF16),
        ],
        compiler_params=pltpu.CompilerParams(vmem_limit_bytes=60 * MIB),
        name="pack_shares",
    )(places, *squares, up, down, tags, *(vector[None] for vector in vectors))


def tie(*values):
    return lax.optimization_barrier(values)


def standing():
    place = lax.axis_index("seq")
    return jnp.stack([lax.axis_index("fsdp"), place // 2, place % 2]).astype(jnp.int32)


def swapped(array, mask):
    size = lax.axis_size("seq")
    return lax.ppermute(array, "seq", [(i, i ^ mask) for i in range(size)])


def turned(array, by):
    size = lax.axis_size("fsdp")
    return lax.ppermute(array, "fsdp", [(i, (i + by) % size) for i in range(size)])


def around(share):
    return [share] + [turned(share, k) for k in range(1, lax.axis_size("fsdp"))]


def across(array, chips):
    return [array] + [swapped(array, 2 * m) for m in range(1, chips)]


def other_core(arrays):
    return [swapped(array, 1) for array in arrays]


def by_shares(block):
    return lax.axis_size("seq") == 8 and block % 128 == 0


def eighth_row(chip, core, m, t):
    return (chip ^ m) * 2 + (core ^ t)


def quarter_row(chip, core, m, t, bit):
    return (core ^ t) * 2 + (((chip >> bit) & 1) ^ m)


def assemble(where_ref, piece_refs, full_ref):
    half = len(piece_refs) // 2
    shards, rows, columns = piece_refs[0].shape
    quarters = columns < full_ref.shape[1]
    block = full_ref.shape[0] // shards
    for number, piece_ref in enumerate(piece_refs):
        t, m = divmod(number, half)
        lane = 0
        if quarters:
            bit, m = divmod(m, 2)
            lane = bit * columns
            place = quarter_row(where_ref[1], where_ref[2], m, t, bit)
        else:
            place = eighth_row(where_ref[1], where_ref[2], m, t)
        for k in range(shards):
            shard = lax.rem(where_ref[0] + shards - k, shards)
            row = pl.multiple_of(shard * block + place * rows, rows)
            full_ref[pl.ds(row, rows), lane : lane + columns] = piece_ref[k]


def split_shares(shards, where_ref, total_ref, keep_ref, send_ref):
    chips, height, _ = keep_ref.shape
    rows = total_ref.shape[0] // (2 * chips * shards)
    block = 2 * chips * rows
    for t, out_ref in enumerate((keep_ref, send_ref)):
        for m in range(chips):
            place = eighth_row(where_ref[1], where_ref[2], m, t)
            for k in range(shards):
                shard = lax.rem(where_ref[0] + k, shards)
                row = pl.multiple_of(shard * block + place * rows, rows)
                out_ref[m, k * rows : (k + 1) * rows, :] = total_ref[pl.ds(row, rows), :].astype(
                    BF16
                )


def add_parts_body(sizes, stacked, *refs):
    ins, outs = refs[: sum(sizes)], refs[sum(sizes) :]
    for number, out_ref in enumerate(outs):
        first, lane = 0, 0
        for size in sizes:
            total = None
            for ref in ins[first : first + size]:
                value = (ref[number] if stacked else ref[...]).astype(F32)
                total = value if total is None else total + value
            columns = total.shape[1]
            out_ref[:, lane : lane + columns] = total.astype(BF16)
            first, lane = first + size, lane + columns


def add_parts(groups, tile, name):
    arrays = [array for group in groups for array in group]
    parts, rows = arrays[0].shape[:2]
    columns = sum(group[0].shape[2] for group in groups)
    return pl.pallas_call(
        functools.partial(add_parts_body, [len(group) for group in groups], True),
        grid=(rows // tile,),
        in_specs=[
            pl.BlockSpec((parts, tile, array.shape[2]), lambda i: (0, i, 0)) for array in arrays
        ],
        out_specs=[pl.BlockSpec((tile, columns), lambda i: (i, 0))] * parts,
        out_shape=[jax.ShapeDtypeStruct((rows, columns), BF16)] * parts,
        compiler_params=pltpu.CompilerParams(vmem_limit_bytes=48 * MIB),
        name=name,
    )(*arrays)


def reduce_whole(grad):
    return lax.psum(lax.psum_scatter(grad, "fsdp", scatter_dimension=0, tiled=True), "seq")


def collect(where_ref, refs, full_ref):
    if full_ref.shape[0] == refs[0].shape[0]:
        lane = 0
        for ref in refs:
            columns = ref.shape[1]
            full_ref[:, lane : lane + columns] = ref[...].astype(F32)
            lane += columns
        return
    half = len(refs) // 2
    rows = refs[0].shape[0]
    for number, ref in enumerate(refs):
        t, m = divmod(number, half)
        row = eighth_row(where_ref[1], where_ref[2], m, t) * rows
        full_ref[pl.ds(pl.multiple_of(row, rows), rows), :] = ref[...].astype(F32)


def copy_feed(full_ref, shards, outs):
    up_ref, down_ref = outs
    block = full_ref.shape[0]
    chunks = down_ref.shape[0] // block
    for part in range(chunks):
        for shard in range(shards):
            here = part * 512 + shard * block
            there = (shard * chunks + part) * block
            up_ref[:, there : there + block] = full_ref[:, here : here + block]
        late = 512 * (chunks + part)
        down_ref[part * block : (part + 1) * block, :] = full_ref[:, late : late + 512]


def copy_attention(full_ref, shards, outs):
    squares, vectors, tag_ref = outs[:8], outs[8:-1], outs[-1]
    block = full_ref.shape[0]
    for number, square_ref in enumerate(squares):
        lane = 512 * ((number + 5) % 8)
        square_ref[...] = full_ref[:, lane : lane + 512]
    for row, vector_ref in enumerate(vectors):
        vector_ref[...] = full_ref[row : row + 1, 4096 : 4096 + block]
    tag_ref[...] = full_ref[TAG_ROW : TAG_ROW + tag_ref.shape[0], 4096 : 4096 + block]


def finish_body(copy, shards, count, where_ref, *refs):
    ins, outs, full_ref = refs[:count], refs[count:-1], refs[-1]
    collect(where_ref, ins, full_ref)
    copy(full_ref, shards, outs)


def finish(copy, name, where, shards, block, columns, pieces, shapes):
    vmem = pl.BlockSpec(memory_space=pltpu.VMEM)
    return pl.pallas_call(
        functools.partial(finish_body, copy, shards, len(pieces)),
        in_specs=[pl.BlockSpec(memory_space=pltpu.SMEM)] + [vmem] * len(pieces),
        out_specs=[vmem] * len(shapes),
        out_shape=[jax.ShapeDtypeStruct(shape, F32) for shape in shapes],
        scratch_shapes=[pltpu.VMEM((block, columns), F32)],
        compiler_params=pltpu.CompilerParams(vmem_limit_bytes=48 * MIB),
        name=name,
    )(where, *pieces)


def local_facts(seg_ids, keep_mask, pair_tags, cut_lo, cut_hi, base, rows):
    sentences = pair_tags.shape[1]
    ids = jnp.arange(sentences, dtype=jnp.int32)
    starts = jnp.sum(seg_ids[:, :, None] < ids, 1, dtype=jnp.int32)
    ends = jnp.sum(seg_ids[:, :, None] <= ids, 1, dtype=jnp.int32)
    half = (ends - starts - 1) // 2
    spare = ((0, 0), (0, LANES - sentences))
    lower = jnp.pad(starts + jnp.minimum(cut_lo, half), spare)
    upper = jnp.pad(ends - jnp.minimum(cut_hi, half), spare)
    edge = ((0, 0), (MAXLEN, MAXLEN))
    width = rows + 2 * MAXLEN
    seg = lax.dynamic_slice_in_dim(jnp.pad(seg_ids, edge, constant_values=-1), base, width, 1)
    keep = lax.dynamic_slice_in_dim(jnp.pad(keep_mask, edge), base, width, 1)
    lanes = jnp.arange(LANES, dtype=jnp.int32)
    hot = seg[:, :, None] == lanes
    place = base - MAXLEN + jnp.arange(width, dtype=jnp.int32)[None, :, None]
    inside = (place >= lower[:, None, :]) & (place < upper[:, None, :])
    near = MAXLEN + rows
    seen = (keep[:, :near] == 1) | (jnp.arange(near) >= MAXLEN)
    self_bias = jnp.where(hot[:, :near] & seen[:, :, None], 0.0, MASKED).astype(BF16)
    cross_bias = jnp.where(inside, 0.0, MASKED).astype(BF16)
    spot = jnp.arange(rows, dtype=jnp.int32)
    earlier = (spot[None, :] < spot[:, None]) & (keep[:, None, MAXLEN:near] == 1)
    own_bias = jnp.where(earlier | (spot[None, :] == spot[:, None]), 0.0, MASKED).astype(F32)
    tag_rows = TAG_ROW + pair_tags
    tags = (tag_rows[:, None, :] == jnp.arange(SMALL_ROWS, dtype=jnp.int32)[:, None]).astype(BF16)
    tags = jnp.pad(tags, ((0, 0), (0, 0), (0, LANES - sentences)))
    return hot.astype(BF16), self_bias, cross_bias, own_bias, tags


def shifted(shard, by):
    size = lax.axis_size("seq")
    pairs = [(i, i + by) for i in range(size) if 0 <= i + by < size]
    return lax.ppermute(shard, "seq", pairs)


def on_device(
    inputs,
    encoded,
    cotangent,
    seg_ids,
    keep_mask,
    pair_tags,
    cut_lo,
    cut_hi,
    w_query,
    w_key,
    w_value,
    w_out,
    c_query,
    c_key,
    c_value,
    c_out,
    w_up,
    w_down,
    gain_one,
    bias_one,
    gain_two,
    bias_two,
    gain_three,
    bias_three,
    tag_table,
):
    batch, rows, _ = inputs.shape
    shards = lax.axis_size("fsdp")
    block = w_query.shape[0]
    chunks = w_down.shape[0] // block
    base = lax.axis_index("seq") * rows
    stepped = by_shares(block)
    places = lax.axis_size("seq")
    chips = places // 2
    where = standing()
    inputs_before = shifted(inputs, 1)
    encoded_after = shifted(encoded, -1)

    down_blocks = w_down.reshape(chunks, block, 512)
    vectors = (gain_one, bias_one, gain_two, bias_two, gain_three, bias_three)
    squares = (w_query, w_key, w_value, w_out, c_query, c_key, c_value, c_out)
    if stepped:
        quarters = [quarter_row(where[1], where[2], 0, 0, bit) for bit in (0, 1)]
        place = jnp.stack([lax.axis_index("seq"), *quarters]).astype(jnp.int32)
        share_one, share_two, share_three = pack_shares(
            place, chunks, shards, squares, w_up, down_blocks, tag_table, vectors
        )
        share_one, share_two, share_three, inputs_before, encoded_after = tie(
            share_one, share_two, share_three, inputs_before, encoded_after
        )
        line_one = jnp.stack(around(share_one))
        line_two = jnp.stack(around(share_two))
        line_one, share_three, seg_ids, keep_mask = tie(line_one, share_three, seg_ids, keep_mask)
        line_three = around(share_three)
        plane_one = across(line_one, chips)
        plane_one, line_two, encoded = tie(plane_one, line_two, encoded)
        full_one = plane_one + other_core(plane_one)
        plane_two = across(line_two, chips)
    else:
        small = jnp.concatenate([jnp.stack(vectors), tag_table], 0)
        small = jnp.pad(small, ((0, block - small.shape[0]), (0, LANES - small.shape[1])))
        up = w_up.reshape(block, shards, chunks, block).swapaxes(1, 2).reshape(block, -1)
        down = down_blocks.swapaxes(0, 1).reshape(block, -1)
        full_one, full_two, full_three = [
            [lax.all_gather(jnp.concatenate(pack, 1), "fsdp", axis=0, tiled=True)]
            for pack in ((*squares[:3], small), squares[3:], (up, down))
        ]

    encoded_before = shifted(encoded, 1)
    hot, self_bias, cross_bias, own_bias, tags = local_facts(
        seg_ids, keep_mask, pair_tags, cut_lo, cut_hi, base, rows
    )
    near, wide = MAXLEN + rows, 2 * MAXLEN + rows

    def tokens(count, kind, width=512):
        return ((batch, count, width), kind)

    self_kept = run_steps(
        functools.partial(self_forward, shards),
        "self_forward",
        8,
        where,
        (inputs_before, inputs, hot, tags, self_bias, own_bias),
        (),
        (full_one,),
        (
            tokens(rows, F32),
            tokens(near, BF16),
            tokens(rows, BF16),
            tokens(near, BF16),
            tokens(near, BF16),
            tokens(rows, F32),
            tokens(rows, F32),
            ((batch, HEADS, rows, near), BF16),
        ),
        (((SMALL_ROWS, 512), F32),),
    )
    if stepped:
        self_kept, plane_two, line_three = tie(self_kept, plane_two, line_three)
        full_two = plane_two + other_core(plane_two)
        middle = line_three[0].shape[1] // 2
        up_line = jnp.stack([piece[:, :middle] for piece in line_three])
        down_line = jnp.stack([piece[:, middle:] for piece in line_three])
        full_two, up_line, down_line = tie(full_two, up_line, down_line)
        plane_three = [up_line, swapped(up_line, 2), down_line, swapped(down_line, 4)]
    start, start_low, s_q, s_k, s_v, s_mix, s_inv, s_exps, smalls = self_kept
    cross_kept = run_steps(
        cross_forward,
        "cross_forward",
        13,
        where,
        (start, s_mix, encoded_before, encoded, encoded_after, hot, cross_bias),
        (smalls,),
        (full_two,),
        (
            tokens(rows, BF16),
            tokens(rows, F32),
            tokens(rows, F32, LANES),
            tokens(rows, BF16),
            tokens(wide, BF16),
            tokens(wide, BF16),
            tokens(rows, F32),
            tokens(rows, F32),
            ((batch, HEADS, rows, wide), BF16),
            tokens(rows, F32),
            tokens(rows, F32),
            tokens(rows, F32, LANES),
        ),
        (),
    )
    if stepped:
        cross_kept, plane_three = tie(cross_kept, plane_three)
        full_three = plane_three + other_core(plane_three)
    (
        norm_low,
        unit_one,
        scale_one,
        c_q,
        c_k,
        c_v,
        c_mix,
        c_inv,
        c_exps,
        normed_two,
        unit_two,
        scale_two,
    ) = cross_kept
    count = batch * rows
    hidden = 512 * chunks

    def flat(array):
        return array.reshape(count, array.shape[-1])

    vmem = pl.BlockSpec(memory_space=pltpu.VMEM)
    three_specs = grad_specs(block, 2 * hidden)
    feed_scratch = [
        pltpu.VMEM((count, hidden), BF16),
        pltpu.VMEM((count, hidden), F32),
        pltpu.VMEM((512, 2 * hidden), BF16),
    ]
    if len(full_three) > 1:
        feed_scratch.append(pltpu.VMEM((512, 2 * hidden), BF16))
    output, d_two, feed_sums, *grad_three = pl.pallas_call(
        functools.partial(feed_both, shards, len(full_three), len(three_specs)),
        in_specs=[pl.BlockSpec(memory_space=pltpu.SMEM)] + [vmem] * (5 + len(full_three)),
        out_specs=[vmem] * (3 + len(three_specs)),
        out_shape=[
            jax.ShapeDtypeStruct((count, 512), BF16),
            jax.ShapeDtypeStruct((count, 512), F32),
            jax.ShapeDtypeStruct((SMALL_ROWS, 512), F32),
            *(jax.ShapeDtypeStruct(*spec) for spec in three_specs),
        ],
        scratch_shapes=feed_scratch,
        compiler_params=pltpu.CompilerParams(vmem_limit_bytes=48 * MIB),
        cost_estimate=busy(13),
        name="feed_both",
    )(
        where,
        flat(normed_two),
        flat(unit_two),
        flat(scale_two),
        flat(cotangent),
        smalls,
        *full_three,
    )
    if stepped:
        three_got = swapped(grad_three[1], 1)
    cross_back = run_steps(
        functools.partial(cross_backward, shards),
        "cross_backward",
        20,
        where,
        (
            d_two.reshape(batch, rows, 512),
            s_mix,
            encoded_before,
            encoded,
            encoded_after,
            norm_low,
            unit_one,
            scale_one,
            c_q,
            c_k,
            c_v,
            c_mix,
            c_inv,
            c_exps,
        ),
        (smalls,),
        (full_two,),
        (
            tokens(rows, F32),
            tokens(rows, BF16),
            tokens(MAXLEN, BF16),
            tokens(rows, F32),
            tokens(MAXLEN, BF16),
        ),
        (((SMALL_ROWS, 512), F32), *grad_specs(block, 2560)),
        (pltpu.VMEM((512, 2560), F32),),
    )
    if stepped:
        cross_back, three_got = tie(cross_back, three_got)
        three_parts = add_parts([[grad_three[0], three_got]], 16, "feed_cores")
        cross_back, three_parts = tie(cross_back, three_parts)
        three_parts = [three_parts[0]] + [
            swapped(three_parts[m], 2 * m) for m in range(1, chips)
        ]
    d_one, d_self_mix, source_before, source_here, source_after, cross_sums, *grad_two = cross_back
    if stepped:
        two_got = swapped(grad_two[1], 1)
    self_back = run_steps(
        functools.partial(self_backward, shards),
        "self_backward",
        15,
        where,
        (d_one, d_self_mix, start_low, hot, tags, s_q, s_k, s_v, s_mix, s_inv, s_exps),
        (feed_sums, cross_sums),
        (full_one,),
        (tokens(MAXLEN, BF16), tokens(rows, F32)),
        grad_specs(block, 1536 + LANES),
        (pltpu.VMEM((512, 1536 + LANES), F32), pltpu.VMEM((SMALL_ROWS, 512), F32)),
    )
    if stepped:
        self_back, three_parts, two_got = tie(self_back, three_parts, two_got)
    start_before, start_here, *grad_one = self_back
    columns = 2560 + 1536 + LANES
    if stepped:
        eighth = block // places

        def by_shard(array):
            return array.reshape(shards, eighth, array.shape[-1])

        def around_parts(parts):
            return [parts[0][None]] + [turned(parts[k], k)[None] for k in range(1, shards)]

        one_got = swapped(grad_one[1], 1)
        three_parts = add_parts([[by_shard(part) for part in three_parts]], eighth, "feed_chips")
        parts = add_parts(
            [[grad_two[0], two_got], [grad_one[0], one_got]], 16, "attention_cores"
        )
        parts, three_parts = tie(parts, three_parts)
        three_parts = around_parts(three_parts)
        parts = [parts[0]] + [swapped(parts[m], 2 * m) for m in range(1, chips)]
        parts, three_parts = tie(parts, three_parts)
        parts = add_parts([[by_shard(part) for part in parts]], eighth, "attention_chips")
        three_share = add_parts([three_parts], eighth, "feed_shards")[0]
        parts, three_share, source_before, source_after, start_before = tie(
            parts, three_share, source_before, source_after, start_before
        )
        parts = around_parts(parts)
        plane = across(three_share, chips)
        three_pieces = plane + other_core(plane)
        share = add_parts([parts], eighth, "attention_shards")[0]
        plane = across(share, chips)
        pieces = plane + other_core(plane)
    else:
        three_pieces = [reduce_whole(grad) for grad in grad_three]
        pieces = [reduce_whole(grad) for grad in (*grad_two, *grad_one)]
    grad_encoded = (source_here + shifted(source_before, -1) + shifted(source_after, 1)).astype(BF16)
    grad_inputs = (start_here + shifted(start_before, -1)).astype(BF16)
    feed_grads = finish(
        copy_feed,
        "feed_finish",
        where,
        shards,
        block,
        2 * hidden,
        three_pieces,
        ((block, hidden), (chunks * block, 512)),
    )
    grads = finish(
        copy_attention,
        "attention_finish",
        where,
        shards,
        block,
        columns,
        pieces,
        ((block, 512),) * 8 + ((1, block),) * TAG_ROW + ((tag_table.shape[0], block),),
    )
    return (
        output.reshape(batch, rows, 512),
        grad_inputs,
        grad_encoded,
        *grads[:8],
        *feed_grads,
        *(part.reshape(block) for part in grads[8:-1]),
        grads[-1],
    )


def solution(mesh):
    rows = P("fsdp", "seq", None)
    by_row = P("fsdp", None)
    vector = P("fsdp")
    tags = P(None, "fsdp")
    return jax.shard_map(
        on_device,
        mesh=mesh,
        in_specs=(rows,) * 3 + (by_row,) * 15 + (vector,) * 6 + (tags,),
        out_specs=(rows,) * 3 + (by_row,) * 10 + (vector,) * 6 + (tags,),
        check_vma=False,
    )
```

```python
import functools

import jax
import jax.numpy as jnp
from jax import lax
from jax.experimental import pallas as pl
from jax.experimental.pallas import tpu as pltpu
from jax.sharding import PartitionSpec as P

HEADS = 8
HEAD_DIM = 64
MAXLEN = 256
LANES = 128
SMALL_ROWS = 32
TAG_ROW = 6
EPSILON = 1e-05
MASKED = -1e30
SCALE = HEAD_DIM ** (-0.5)
BF16 = jnp.bfloat16
F32 = jnp.float32
MIB = 2**20
PER_US = 10**9

NN = (((1,), (0,)), ((), ()))
NT = (((1,), (1,)), ((), ()))
TN = (((0,), (0,)), ((), ()))


def dot(left, right, dims=NN):
    return lax.dot_general(left, right, dims, preferred_element_type=F32)


def lane_ids(rows):
    return lax.broadcasted_iota(jnp.int32, (rows, LANES), 1)


def norm_rows(values_in):
    center = values_in - jnp.mean(values_in, -1, keepdims=True)
    inverse = lax.rsqrt(jnp.mean(center * center, -1, keepdims=True) + EPSILON)
    return center * inverse, inverse


def norm_back(grad_rows, unit_rows, inverse, gain):
    scaled = grad_rows * gain
    centered = (
        scaled
        - jnp.mean(scaled, -1, keepdims=True)
        - unit_rows * jnp.mean(scaled * unit_rows, -1, keepdims=True)
    )
    return inverse * centered


def column_sums(values_in):
    return jnp.sum(values_in, 0, keepdims=True)


def attend(queries, keys, values, query_hot, key_bias, own_bias, exps_ref):
    rows, width = queries.shape[0], keys.shape[0]
    low = lane_ids(rows) < HEAD_DIM
    ones = jnp.ones((width, LANES), BF16)
    mixes, inverses = [], []
    for pair in range(HEADS // 2):
        cols = slice(LANES * pair, LANES * (pair + 1))
        pair_q = queries[:, cols]
        pair_k = jnp.concatenate([keys[:, cols], key_bias], 1)
        pair_v = jnp.concatenate([values[:, cols], ones], 1)
        sums = []
        for half in (0, 1):
            mine = low if half == 0 else ~low
            head_q = jnp.concatenate([jnp.where(mine, pair_q, jnp.zeros_like(pair_q)), query_hot], 1)
            scores = dot(head_q, pair_k, NT)
            if own_bias is not None:
                near = width - rows
                scores = jnp.concatenate([scores[:, :near], scores[:, near:] + own_bias], 1)
            highest = jnp.max(scores, -1, keepdims=True)
            exps = jnp.exp(scores - highest).astype(BF16)
            exps_ref[0, 2 * pair + half] = exps
            sums.append(dot(exps, pair_v))
        inverse = 1.0 / jnp.where(low, sums[0][:, LANES:], sums[1][:, LANES:])
        mixes.append(jnp.where(low, sums[0][:, :LANES], sums[1][:, :LANES]) * inverse)
        inverses.append(inverse)
    return jnp.concatenate(mixes, 1), jnp.concatenate(inverses, 1)


def attend_back(queries, keys, values, exps_ref, mix, inverse, grad_mix):
    rows, width = queries.shape[0], keys.shape[0]
    lane = lane_ids(rows)
    low = lane < HEAD_DIM
    low_wide = lane_ids(width) < HEAD_DIM
    two_ones = jnp.where(lane_ids(width) < 2, 1.0, 0.0).astype(BF16)
    grads_q, grads_k, grads_v = [], [], []
    for pair in range(HEADS // 2):
        cols = slice(LANES * pair, LANES * (pair + 1))
        pair_q, pair_k = queries[:, cols], keys[:, cols]
        pair_v = jnp.concatenate([values[:, cols], two_ones], 1)
        scaled = (grad_mix[:, cols].astype(F32) * inverse[:, cols]).astype(BF16)
        product = scaled.astype(F32) * mix[:, cols]
        found_q, found_k, found_v = [], [], []
        for half in (0, 1):
            mine = low if half == 0 else ~low
            centre = jnp.sum(jnp.where(mine, product, 0.0), -1, keepdims=True)
            coarse = centre.astype(BF16).astype(F32)
            shift = jnp.where(lane == 0, -coarse, jnp.where(lane == 1, coarse - centre, 0.0))
            head_g = jnp.concatenate(
                [jnp.where(mine, scaled, jnp.zeros_like(scaled)), shift.astype(BF16)], 1
            )
            exps = exps_ref[0, 2 * pair + half]
            grad_scores = (exps.astype(F32) * dot(head_g, pair_v, NT)).astype(BF16)
            found_q.append(dot(grad_scores, pair_k))
            found_k.append(dot(grad_scores, pair_q, TN))
            found_v.append(dot(exps, scaled, TN))
        grads_q.append(jnp.where(low, found_q[0], found_q[1]) * SCALE)
        grads_k.append(jnp.where(low_wide, found_k[0], found_k[1]))
        grads_v.append(jnp.where(low_wide, found_v[0], found_v[1]))
    return [jnp.concatenate(part, 1).astype(BF16) for part in (grads_q, grads_k, grads_v)]


def matrix(ref, number, width=512):
    return ref[:, number * width : (number + 1) * width]


def self_forward(
    shards,
    where_ref,
    before_ref,
    here_ref,
    hot_ref,
    tag_ref,
    bias_ref,
    own_ref,
    weight_ref,
    start_ref,
    low_ref,
    q_ref,
    k_ref,
    v_ref,
    mix_ref,
    inv_ref,
    exps_ref,
    small_ref,
    one_ref,
):
    rows = here_ref.shape[1]
    block = 512 // shards

    @pl.when(pl.program_id(0) == 0)
    def _():
        one_ref[...] = weight_ref[...]

    smalls = jnp.concatenate(
        [
            weight_ref[z * block : z * block + SMALL_ROWS, 1536 : 1536 + block]
            for z in range(shards)
        ],
        1,
    )
    small_ref[...] = smalls.astype(F32)
    seg_tags = dot(tag_ref[0], smalls, TN).astype(BF16)
    hot = hot_ref[0, : MAXLEN + rows]
    tokens = jnp.concatenate([before_ref[0], here_ref[0]], 0).astype(F32)
    start = tokens + dot(hot, seg_tags)
    start_ref[0] = start[MAXLEN:]
    start_low = start.astype(BF16)
    low_ref[0] = start_low
    queries = (dot(start_low[MAXLEN:], matrix(weight_ref, 0)).astype(BF16).astype(F32) * SCALE).astype(BF16)
    keys = dot(start_low, matrix(weight_ref, 1)).astype(BF16)
    values = dot(start_low, matrix(weight_ref, 2)).astype(BF16)
    q_ref[0] = queries
    k_ref[0] = keys
    v_ref[0] = values
    mix_ref[0], inv_ref[0] = attend(
        queries, keys, values, hot[MAXLEN:], bias_ref[0], own_ref[0], exps_ref
    )


def cross_forward(
    where_ref,
    start_ref,
    self_mix_ref,
    before_ref,
    here_ref,
    after_ref,
    hot_ref,
    bias_ref,
    small_ref,
    weight_ref,
    norm_low_ref,
    unit_one_ref,
    scale_one_ref,
    q_ref,
    k_ref,
    v_ref,
    mix_ref,
    inv_ref,
    exps_ref,
    normed_ref,
    unit_two_ref,
    scale_two_ref,
    two_ref,
):
    rows = start_ref.shape[1]

    @pl.when(pl.program_id(0) == 0)
    def _():
        two_ref[...] = weight_ref[...]

    source = jnp.concatenate([before_ref[0], here_ref[0], after_ref[0]], 0)
    keys = dot(source, matrix(weight_ref, 2)).astype(BF16)
    values = dot(source, matrix(weight_ref, 3)).astype(BF16)
    k_ref[0] = keys
    v_ref[0] = values
    branch = dot(self_mix_ref[0].astype(BF16), matrix(weight_ref, 0))
    unit_one, scale_one = norm_rows(start_ref[0] + branch)
    unit_one_ref[0] = unit_one
    scale_one_ref[0] = jnp.broadcast_to(scale_one, (rows, LANES))
    normed_one = unit_one * small_ref[0:1] + small_ref[1:2]
    norm_low = normed_one.astype(BF16)
    norm_low_ref[0] = norm_low
    queries = (dot(norm_low, matrix(weight_ref, 1)).astype(BF16).astype(F32) * SCALE).astype(BF16)
    q_ref[0] = queries
    mix, inverse = attend(
        queries, keys, values, hot_ref[0, MAXLEN : MAXLEN + rows], bias_ref[0], None, exps_ref
    )
    mix_ref[0] = mix
    inv_ref[0] = inverse
    branch = dot(mix.astype(BF16), matrix(weight_ref, 4))
    unit_two, scale_two = norm_rows(normed_one + branch)
    unit_two_ref[0] = unit_two
    scale_two_ref[0] = jnp.broadcast_to(scale_two, (rows, LANES))
    normed_ref[0] = unit_two * small_ref[2:3] + small_ref[3:4]


GELU_A = 0.7978845608028654
GELU_B = 0.044715


def feed_both(
    shards,
    pieces,
    grads,
    where_ref,
    normed_ref,
    unit_ref,
    scale_ref,
    cotangent_ref,
    small_ref,
    *rest,
):
    piece_refs, rest = rest[:pieces], rest[pieces:]
    out_ref, back_ref, sums_ref, *rest = rest
    grad_refs, rest = rest[:grads], rest[grads:]
    act_ref, slope_ref, grad_ref, *rest = rest
    weight_ref = piece_refs[0]
    if pieces > 1:
        (weight_ref,) = rest
        assemble(where_ref, piece_refs, weight_ref)
    normed = normed_ref[...]
    normed_low = normed.astype(BF16)
    chunks = weight_ref.shape[1] // 1024
    feed = normed
    for part in range(chunks):
        cols = slice(512 * part, 512 * (part + 1))
        hidden = dot(normed_low, matrix(weight_ref, part))
        square = hidden * hidden
        bend = jnp.tanh(hidden * (GELU_A + GELU_A * GELU_B * square))
        rise = 0.5 + 0.5 * bend
        act = (hidden * rise).astype(BF16)
        act_ref[:, cols] = act
        slope_ref[:, cols] = rise + rise * (1.0 - bend) * hidden * (
            GELU_A + 3.0 * GELU_A * GELU_B * square
        )
        feed = feed + dot(act, matrix(weight_ref, chunks + part))
    unit, scale = norm_rows(feed)
    gain = small_ref[4:5]
    out_ref[...] = (unit * gain + small_ref[5:6]).astype(BF16)
    grad = cotangent_ref[...].astype(F32)
    sums_ref[...] = jnp.zeros_like(sums_ref)
    sums_ref[4:5] = column_sums(grad * unit)
    sums_ref[5:6] = column_sums(grad)
    d_three = norm_back(grad, unit, scale, gain)
    d_feed = d_three.astype(BF16)
    total = d_three
    for part in range(chunks):
        cols = slice(512 * part, 512 * (part + 1))
        late = slice(512 * (chunks + part), 512 * (chunks + part + 1))
        grad_ref[:, late] = dot(act_ref[:, cols], d_feed, TN).astype(BF16)
        d_hidden = (
            slope_ref[:, cols] * dot(d_feed, matrix(weight_ref, chunks + part), NT)
        ).astype(BF16)
        grad_ref[:, cols] = dot(normed_low, d_hidden, TN).astype(BF16)
        total = total + dot(d_hidden, matrix(weight_ref, part), NT)
    unit_two = unit_ref[...]
    sums_ref[2:3] = column_sums(total * unit_two)
    sums_ref[3:4] = column_sums(total)
    back_ref[...] = norm_back(total, unit_two, scale_ref[:, 0:1], small_ref[2:3])
    give(shards, where_ref, grad_ref, grad_refs)


def cross_attend_back(
    where_ref,
    back_ref,
    q_ref,
    k_ref,
    v_ref,
    mix_ref,
    inv_ref,
    exps_ref,
    weight_ref,
    d_q_ref,
    d_k_ref,
    d_v_ref,
):
    d_mix = dot(back_ref[0].astype(BF16), weight_ref[...], NT).astype(BF16)
    d_q_ref[0], d_k_ref[0], d_v_ref[0] = attend_back(
        q_ref[0], k_ref[0], v_ref[0], exps_ref, mix_ref[0], inv_ref[0], d_mix
    )


def add_columns(total_ref, number, value):
    cols = slice(512 * number, 512 * (number + 1))
    total_ref[:, cols] = total_ref[:, cols] + value


def cross_backward(
    shards,
    where_ref,
    back_ref,
    mix_ref,
    self_mix_ref,
    before_ref,
    here_ref,
    after_ref,
    norm_low_ref,
    unit_ref,
    scale_ref,
    d_q_ref,
    d_k_ref,
    d_v_ref,
    small_ref,
    weight_ref,
    one_ref,
    d_mix_ref,
    source_before_ref,
    source_here_ref,
    source_after_ref,
    sums_ref,
    *rest,
):
    *grad_refs, total_ref = rest
    step = pl.program_id(0)
    rows = here_ref.shape[1]

    @pl.when(step == 0)
    def _():
        total_ref[...] = jnp.zeros_like(total_ref)
        sums_ref[...] = jnp.zeros_like(sums_ref)

    d_two = back_ref[0]
    d_q, d_k, d_v = d_q_ref[0], d_k_ref[0], d_v_ref[0]
    add_columns(total_ref, 4, dot(mix_ref[0].astype(BF16), d_two.astype(BF16), TN))
    source = jnp.concatenate([before_ref[0], here_ref[0], after_ref[0]], 0)
    add_columns(total_ref, 2, dot(source, d_k, TN))
    add_columns(total_ref, 3, dot(source, d_v, TN))
    d_source = dot(d_k, matrix(weight_ref, 2), NT) + dot(d_v, matrix(weight_ref, 3), NT)
    source_before_ref[0] = d_source[:MAXLEN].astype(BF16)
    source_here_ref[0] = d_source[MAXLEN : MAXLEN + rows]
    source_after_ref[0] = d_source[MAXLEN + rows :].astype(BF16)
    add_columns(total_ref, 1, dot(norm_low_ref[0], d_q, TN))
    total = d_two + dot(d_q, matrix(weight_ref, 1), NT)
    unit = unit_ref[0]
    sums_ref[0:1] = sums_ref[0:1] + column_sums(total * unit)
    sums_ref[1:2] = sums_ref[1:2] + column_sums(total)
    d_one = norm_back(total, unit, scale_ref[0, :, 0:1], small_ref[0:1])
    one_ref[0] = d_one
    d_one_low = d_one.astype(BF16)
    add_columns(total_ref, 0, dot(self_mix_ref[0].astype(BF16), d_one_low, TN))
    d_mix_ref[0] = dot(d_one_low, matrix(weight_ref, 0), NT).astype(BF16)

    @pl.when(step == pl.num_programs(0) - 1)
    def _():
        give(shards, where_ref, total_ref, grad_refs)


def self_backward(
    shards,
    where_ref,
    one_ref,
    d_mix_ref,
    low_ref,
    hot_ref,
    tag_ref,
    q_ref,
    k_ref,
    v_ref,
    mix_ref,
    inv_ref,
    exps_ref,
    feed_sums_ref,
    cross_sums_ref,
    weight_ref,
    before_ref,
    here_ref,
    *rest,
):
    *grad_refs, total_ref, sums_ref = rest
    step = pl.program_id(0)
    rows = one_ref.shape[1]

    @pl.when(step == 0)
    def _():
        total_ref[...] = jnp.zeros_like(total_ref)
        sums_ref[...] = feed_sums_ref[...] + cross_sums_ref[...]

    def add(number, value):
        cols = slice(512 * number, 512 * (number + 1))
        total_ref[:, cols] = total_ref[:, cols] + value

    d_one = one_ref[0]
    d_mix = d_mix_ref[0]
    d_q, d_k, d_v = attend_back(
        q_ref[0], k_ref[0], v_ref[0], exps_ref, mix_ref[0], inv_ref[0], d_mix
    )
    start_low = low_ref[0]
    add(0, dot(start_low[MAXLEN:], d_q, TN))
    add(1, dot(start_low, d_k, TN))
    add(2, dot(start_low, d_v, TN))
    d_start = dot(d_k, matrix(weight_ref, 1), NT) + dot(d_v, matrix(weight_ref, 2), NT)
    d_before = d_start[:MAXLEN].astype(BF16)
    d_here = d_start[MAXLEN:] + d_one + dot(d_q, matrix(weight_ref, 0), NT)
    before_ref[0] = d_before
    here_ref[0] = d_here
    both = jnp.concatenate([d_before, d_here.astype(BF16)], 0)
    seg_sums = dot(hot_ref[0, : MAXLEN + rows], both, TN)
    coarse = seg_sums.astype(BF16)
    fine = (seg_sums - coarse.astype(F32)).astype(BF16)
    sums_ref[...] = sums_ref[...] + dot(tag_ref[0], coarse) + dot(tag_ref[0], fine)

    @pl.when(step == pl.num_programs(0) - 1)
    def _():
        block = 512 // shards
        for z in range(shards):
            total_ref[z * block : z * block + SMALL_ROWS, 1536 : 1536 + block] = sums_ref[
                :, z * block : (z + 1) * block
            ]
        give(shards, where_ref, total_ref, grad_refs)


def busy(micros):
    return pl.CostEstimate(
        flops=micros * PER_US, bytes_accessed=micros * 2 * MIB, transcendentals=0
    )


def per_step(array):
    rest = (0,) * (array.ndim - 1)
    return pl.BlockSpec((1,) + array.shape[1:], lambda step: (step,) + rest)


def whole(array):
    rest = (0,) * array.ndim
    return pl.BlockSpec(array.shape, lambda step: rest)


def run_steps(
    body,
    name,
    micros,
    where,
    stepped,
    fixed,
    weights,
    stepped_outs,
    fixed_outs,
    scratch=(),
    squares=(),
):
    batch = stepped[0].shape[0]
    outs = [jax.ShapeDtypeStruct(*spec) for spec in (*stepped_outs, *fixed_outs)]
    counts = [len(stepped), len(fixed), *(len(pieces) for pieces in weights)]
    outs_count = len(outs)
    whole_scratch = [
        pltpu.VMEM((512, pieces[0].shape[-1]), BF16) for pieces in weights if len(pieces) > 1
    ]

    def called(where_ref, *refs):
        refs = list(refs)

        def take(count):
            taken = refs[:count]
            del refs[:count]
            return taken

        plain = take(counts[0] + counts[1])
        pieces = [take(count) for count in counts[2:]]
        square_refs = take(len(squares))
        outs_refs = take(outs_count)
        own_scratch = take(len(scratch))
        fulls = []
        for piece_refs in pieces:
            if len(piece_refs) == 1:
                fulls.append(piece_refs[0])
                continue
            (full_ref,) = take(1)
            fulls.append(full_ref)

            @pl.when(pl.program_id(0) == 0)
            def _(piece_refs=piece_refs, full_ref=full_ref):
                assemble(where_ref, piece_refs, full_ref)

        body(where_ref, *plain, *fulls, *square_refs, *outs_refs, *own_scratch)

    flat_weights = [piece for pieces in weights for piece in pieces]
    steps = len(stepped_outs)
    return pl.pallas_call(
        called,
        grid=(batch,),
        in_specs=[pl.BlockSpec(memory_space=pltpu.SMEM)]
        + [per_step(a) for a in stepped]
        + [whole(a) for a in (*fixed, *flat_weights)]
        + [pl.BlockSpec((512, 512), lambda step, number=number: (0, number)) for _, number in squares],
        out_specs=[per_step(a) for a in outs[:steps]] + [whole(a) for a in outs[steps:]],
        out_shape=outs,
        scratch_shapes=[*scratch, *whole_scratch],
        compiler_params=pltpu.CompilerParams(vmem_limit_bytes=20 * MIB),
        cost_estimate=busy(micros),
        name=name,
    )(where, *stepped, *fixed, *flat_weights, *(array for array, _ in squares))


def grad_specs(block, columns):
    if not by_shares(block):
        return (((512, columns), BF16),)
    places = lax.axis_size("seq")
    return (((places // 2, 512 // places, columns), BF16),) * 2


def give(shards, where_ref, total_ref, refs):
    if len(refs) == 1:
        refs[0][...] = total_ref[...].astype(BF16)
    else:
        split_shares(shards, where_ref, total_ref, *refs)


def pack_body(chunks, shards, place_ref, *refs):
    ins, (low_ref, small_ref) = refs[:-2], refs[-2:]
    squares, (up_ref, down_ref, tag_ref), vectors = ins[:8], ins[8:11], ins[11:]
    eighth = low_ref.shape[0]
    block = small_ref.shape[0]
    small_ref[...] = jnp.zeros_like(small_ref)
    for row, vector_ref in enumerate(vectors):
        small_ref[row : row + 1, :block] = vector_ref[...].astype(F32)
    small_ref[TAG_ROW : TAG_ROW + tag_ref.shape[0], :block] = tag_ref[...].astype(F32)
    for number in range(3):
        low_ref[:, 512 * number : 512 * (number + 1)] = squares[number][...]
    row = pl.multiple_of(place_ref[0] * eighth, eighth)
    low_ref[:, 1536 : 1536 + LANES] = small_ref[pl.ds(row, eighth), :].astype(BF16)
    for number in range(5):
        lane = 1536 + LANES + 512 * number
        low_ref[:, lane : lane + 512] = squares[3 + number][...]
    for part in range(chunks):
        for shard in range(shards):
            here = (shard * chunks + part) * block
            there = 4096 + LANES + part * 512 + shard * block
            low_ref[:, there : there + block] = up_ref[:, here : here + block]
        lane = 4096 + LANES + 512 * (chunks + part)
        low_ref[:, lane : lane + 512] = down_ref[part]


def pack_shares(places, chunks, shards, squares, up, down, tags, vectors):
    block = squares[0].shape[0]
    eighth = block // 8
    columns = 4096 + LANES + 2 * up.shape[1]

    def rows_at(step, place):
        return place[0], 0

    return pl.pallas_call(
        functools.partial(pack_body, chunks, shards),
        grid_spec=pltpu.PrefetchScalarGridSpec(
            num_scalar_prefetch=1,
            grid=(1,),
            in_specs=[pl.BlockSpec((eighth, 512), rows_at)] * 8
            + [
                pl.BlockSpec((eighth, up.shape[1]), rows_at),
                pl.BlockSpec((chunks, eighth, 512), lambda step, place: (0, place[0], 0)),
                pl.BlockSpec(tags.shape, lambda step, place: (0, 0)),
            ]
            + [pl.BlockSpec((1, block), lambda step, place: (0, 0))] * len(vectors),
            out_specs=pl.BlockSpec((eighth, columns), lambda step, place: (0, 0)),
            scratch_shapes=[pltpu.VMEM((block, LANES), F32)],
        ),
        out_shape=jax.ShapeDtypeStruct((eighth, columns), BF16),
        compiler_params=pltpu.CompilerParams(vmem_limit_bytes=60 * MIB),
        name="pack_shares",
    )(places, *squares, up, down, tags, *(vector[None] for vector in vectors))


def tie(*values):
    return lax.optimization_barrier(values)


def standing():
    place = lax.axis_index("seq")
    return jnp.stack([lax.axis_index("fsdp"), place // 2, place % 2]).astype(jnp.int32)


def swapped(array, mask):
    size = lax.axis_size("seq")
    return lax.ppermute(array, "seq", [(i, i ^ mask) for i in range(size)])


def turned(array, by):
    size = lax.axis_size("fsdp")
    return lax.ppermute(array, "fsdp", [(i, (i + by) % size) for i in range(size)])


def around(share):
    return [share] + [turned(share, k) for k in range(1, lax.axis_size("fsdp"))]


def across(array, chips):
    return [array] + [swapped(array, 2 * m) for m in range(1, chips)]


def other_core(arrays):
    return [swapped(array, 1) for array in arrays]


def across_parts(parts):
    return [parts[0]] + [swapped(parts[m], 2 * m) for m in range(1, len(parts))]


def around_parts(parts):
    return [parts[0][None]] + [turned(parts[k], k)[None] for k in range(1, len(parts))]


def by_shard(arrays, shards):
    return [array.reshape(shards, -1, array.shape[-1]) for array in arrays]


def by_shares(block):
    return lax.axis_size("seq") == 8 and lax.axis_size("fsdp") == 4 and block % 128 == 0


def eighth_row(chip, core, m, t):
    return (chip ^ m) * 2 + (core ^ t)


PLAIN_PIECES = ((0, 0), (1, 0), (2, 0), (3, 0))
FEED_PIECES = ((0, 0), (1, 0), (2, 0), (3, 0), (0, 1), (2, 1), (1, 1), (3, 1))


def assemble(where_ref, piece_refs, full_ref):
    pieces = []
    for ref in piece_refs:
        pieces += [ref] if len(ref.shape) == 3 else [ref.at[i] for i in range(ref.shape[0])]
    shards, rows, columns = pieces[0].shape
    block = full_ref.shape[0] // shards
    places = FEED_PIECES if columns < full_ref.shape[1] else PLAIN_PIECES
    for number, piece_ref in enumerate(pieces):
        t, index = divmod(number, len(places))
        m, half = places[index]
        place = eighth_row(where_ref[1], where_ref[2], m, t)
        for k in range(shards):
            shard = lax.rem(where_ref[0] + shards - k, shards)
            row = pl.multiple_of(shard * block + place * rows, rows)
            full_ref[pl.ds(row, rows), half * columns : (half + 1) * columns] = piece_ref[k]


def split_shares(shards, where_ref, total_ref, keep_ref, send_ref):
    chips, height, _ = keep_ref.shape
    rows = total_ref.shape[0] // (2 * chips * shards)
    block = 2 * chips * rows
    for t, out_ref in enumerate((keep_ref, send_ref)):
        for m in range(chips):
            place = eighth_row(where_ref[1], where_ref[2], m, t)
            for k in range(shards):
                shard = lax.rem(where_ref[0] + k, shards)
                row = pl.multiple_of(shard * block + place * rows, rows)
                out_ref[m, k * rows : (k + 1) * rows, :] = total_ref[pl.ds(row, rows), :].astype(
                    BF16
                )


def add_parts_body(sizes, stacked, *refs):
    ins, outs = refs[: sum(sizes)], refs[sum(sizes) :]
    for number, out_ref in enumerate(outs):
        first, lane = 0, 0
        for size in sizes:
            total = None
            for ref in ins[first : first + size]:
                value = (ref[number] if stacked else ref[...]).astype(F32)
                total = value if total is None else total + value
            columns = total.shape[1]
            out_ref[:, lane : lane + columns] = total.astype(BF16)
            first, lane = first + size, lane + columns


def add_parts(groups, tile, name):
    arrays = [array for group in groups for array in group]
    parts, rows = arrays[0].shape[:2]
    columns = sum(group[0].shape[2] for group in groups)
    return pl.pallas_call(
        functools.partial(add_parts_body, [len(group) for group in groups], True),
        grid=(rows // tile,),
        in_specs=[
            pl.BlockSpec((parts, tile, array.shape[2]), lambda i: (0, i, 0)) for array in arrays
        ],
        out_specs=[pl.BlockSpec((tile, columns), lambda i: (i, 0))] * parts,
        out_shape=[jax.ShapeDtypeStruct((rows, columns), BF16)] * parts,
        compiler_params=pltpu.CompilerParams(vmem_limit_bytes=20 * MIB),
        name=name,
    )(*arrays)


def reduce_whole(grad):
    return lax.psum(lax.psum_scatter(grad, "fsdp", scatter_dimension=0, tiled=True), "seq")


def collect(where_ref, refs, full_ref):
    if full_ref.shape[0] == refs[0].shape[0]:
        lane = 0
        for ref in refs:
            columns = ref.shape[1]
            full_ref[:, lane : lane + columns] = ref[...].astype(F32)
            lane += columns
        return
    half = len(refs) // 2
    rows = refs[0].shape[0]
    for number, ref in enumerate(refs):
        t, m = divmod(number, half)
        row = eighth_row(where_ref[1], where_ref[2], m, t) * rows
        full_ref[pl.ds(pl.multiple_of(row, rows), rows), :] = ref[...].astype(F32)


def finish_body(shards, count, where_ref, *refs):
    ins, outs, full_ref = refs[:count], list(refs[count:-1]), refs[-1]
    collect(where_ref, ins, full_ref)
    block = full_ref.shape[0]
    squares, (up_ref, down_ref), vectors, tag_ref = outs[:8], outs[8:10], outs[10:-1], outs[-1]
    chunks = down_ref.shape[0] // block
    for part in range(chunks):
        for shard in range(shards):
            here = part * 512 + shard * block
            there = (shard * chunks + part) * block
            up_ref[:, there : there + block] = full_ref[:, here : here + block]
        late = 512 * (chunks + part)
        down_ref[part * block : (part + 1) * block, :] = full_ref[:, late : late + 512]
    cross = 1024 * chunks
    late = cross + 5 * 512
    for number in range(8):
        lane = late + 512 * number if number < 3 else cross + 512 * (number - 3)
        squares[number][...] = full_ref[:, lane : lane + 512]
    lane = late + 3 * 512
    for row, vector_ref in enumerate(vectors):
        vector_ref[...] = full_ref[row : row + 1, lane : lane + block]
    tag_ref[...] = full_ref[TAG_ROW : TAG_ROW + tag_ref.shape[0], lane : lane + block]


def finish(where, shards, block, columns, pieces, shapes):
    vmem = pl.BlockSpec(memory_space=pltpu.VMEM)
    return pl.pallas_call(
        functools.partial(finish_body, shards, len(pieces)),
        in_specs=[pl.BlockSpec(memory_space=pltpu.SMEM)] + [vmem] * len(pieces),
        out_specs=[vmem] * len(shapes),
        out_shape=[jax.ShapeDtypeStruct(shape, F32) for shape in shapes],
        scratch_shapes=[pltpu.VMEM((block, columns), F32)],
        compiler_params=pltpu.CompilerParams(vmem_limit_bytes=20 * MIB),
        name="finish",
    )(where, *pieces)


def local_facts(seg_ids, keep_mask, pair_tags, cut_lo, cut_hi, base, rows):
    sentences = pair_tags.shape[1]
    ids = jnp.arange(sentences, dtype=jnp.int32)
    starts = jnp.sum(seg_ids[:, :, None] < ids, 1, dtype=jnp.int32)
    ends = jnp.sum(seg_ids[:, :, None] <= ids, 1, dtype=jnp.int32)
    half = (ends - starts - 1) // 2
    spare = ((0, 0), (0, LANES - sentences))
    lower = jnp.pad(starts + jnp.minimum(cut_lo, half), spare)
    upper = jnp.pad(ends - jnp.minimum(cut_hi, half), spare)
    edge = ((0, 0), (MAXLEN, MAXLEN))
    width = rows + 2 * MAXLEN
    seg = lax.dynamic_slice_in_dim(jnp.pad(seg_ids, edge, constant_values=-1), base, width, 1)
    keep = lax.dynamic_slice_in_dim(jnp.pad(keep_mask, edge), base, width, 1)
    lanes = jnp.arange(LANES, dtype=jnp.int32)
    hot = seg[:, :, None] == lanes
    place = base - MAXLEN + jnp.arange(width, dtype=jnp.int32)[None, :, None]
    inside = (place >= lower[:, None, :]) & (place < upper[:, None, :])
    near = MAXLEN + rows
    seen = (keep[:, :near] == 1) | (jnp.arange(near) >= MAXLEN)
    self_bias = jnp.where(hot[:, :near] & seen[:, :, None], 0.0, MASKED).astype(BF16)
    cross_bias = jnp.where(inside, 0.0, MASKED).astype(BF16)
    spot = jnp.arange(rows, dtype=jnp.int32)
    earlier = (spot[None, :] < spot[:, None]) & (keep[:, None, MAXLEN:near] == 1)
    own_bias = jnp.where(earlier | (spot[None, :] == spot[:, None]), 0.0, MASKED).astype(F32)
    tag_rows = TAG_ROW + pair_tags
    tags = (tag_rows[:, None, :] == jnp.arange(SMALL_ROWS, dtype=jnp.int32)[:, None]).astype(BF16)
    tags = jnp.pad(tags, ((0, 0), (0, 0), (0, LANES - sentences)))
    return hot.astype(BF16), self_bias, cross_bias, own_bias, tags


def shifted(shard, by):
    size = lax.axis_size("seq")
    pairs = [(i, i + by) for i in range(size) if 0 <= i + by < size]
    return lax.ppermute(shard, "seq", pairs)


def on_device(
    inputs,
    encoded,
    cotangent,
    seg_ids,
    keep_mask,
    pair_tags,
    cut_lo,
    cut_hi,
    w_query,
    w_key,
    w_value,
    w_out,
    c_query,
    c_key,
    c_value,
    c_out,
    w_up,
    w_down,
    gain_one,
    bias_one,
    gain_two,
    bias_two,
    gain_three,
    bias_three,
    tag_table,
):
    batch, rows, _ = inputs.shape
    shards = lax.axis_size("fsdp")
    block = w_query.shape[0]
    chunks = w_down.shape[0] // block
    base = lax.axis_index("seq") * rows
    stepped = by_shares(block)
    places = lax.axis_size("seq")
    chips = places // 2
    where = standing()
    both_before = shifted(jnp.concatenate([inputs, encoded], 0), 1)
    encoded_after = shifted(encoded, -1)

    down_blocks = w_down.reshape(chunks, block, 512)
    vectors = (gain_one, bias_one, gain_two, bias_two, gain_three, bias_three)
    squares = (w_query, w_key, w_value, w_out, c_query, c_key, c_value, c_out)
    eighth = block // places
    if stepped:
        place = lax.axis_index("seq").astype(jnp.int32)[None]
        share = pack_shares(
            place, chunks, shards, squares, w_up, down_blocks, tag_table, vectors
        )
        line = around(share)
        bounds = (0, 1536 + LANES, 4096 + LANES, 4096 + LANES + 512 * chunks, share.shape[1])
        line_one, line_two, up_line, down_line = [
            jnp.stack([part[:, first:last] for part in line])
            for first, last in zip(bounds[:-1], bounds[1:])
        ]
        line_one, line_two, up_line, down_line, seg_ids, keep_mask, both_before, encoded_after = tie(
            line_one, line_two, up_line, down_line, seg_ids, keep_mask, both_before, encoded_after
        )
        plane_one = across(line_one, chips)
        plane_one, line_two, up_line, down_line = tie(plane_one, line_two, up_line, down_line)
        full_one = plane_one + other_core(plane_one)
        plane_two = across(line_two, chips)
        up_near, down_near = swapped(up_line, 2), swapped(down_line, 4)
    else:
        small = jnp.concatenate([jnp.stack(vectors), tag_table], 0)
        small = jnp.pad(small, ((0, block - small.shape[0]), (0, LANES - small.shape[1])))
        up = w_up.reshape(block, shards, chunks, block).swapaxes(1, 2).reshape(block, -1)
        down = down_blocks.swapaxes(0, 1).reshape(block, -1)
        full_one, full_two, full_feed = [
            [lax.all_gather(jnp.concatenate(pack, 1), "fsdp", axis=0, tiled=True)]
            for pack in ((*squares[:3], small), squares[3:], (up, down))
        ]

    inputs_before, encoded_before = both_before[:batch], both_before[batch:]
    hot, self_bias, cross_bias, own_bias, tags = local_facts(
        seg_ids, keep_mask, pair_tags, cut_lo, cut_hi, base, rows
    )
    near, wide = MAXLEN + rows, 2 * MAXLEN + rows

    def tokens(count, kind, width=512):
        return ((batch, count, width), kind)

    self_kept = run_steps(
        functools.partial(self_forward, shards),
        "self_forward",
        8,
        where,
        (inputs_before, inputs, hot, tags, self_bias, own_bias),
        (),
        (full_one,),
        (
            tokens(rows, F32),
            tokens(near, BF16),
            tokens(rows, BF16),
            tokens(near, BF16),
            tokens(near, BF16),
            tokens(rows, F32),
            tokens(rows, F32),
            ((batch, HEADS, rows, near), BF16),
        ),
        (((SMALL_ROWS, 512), F32), ((512, 1536 + LANES), BF16)),
    )
    if stepped:
        self_kept, plane_two, up_near, down_near = tie(self_kept, plane_two, up_near, down_near)
        full_two = plane_two + other_core(plane_two)
        up_far = swapped(jnp.stack([up_line, up_near]), 4)
        down_far = swapped(jnp.stack([down_line, down_near]), 2)
    start, start_low, s_q, s_k, s_v, s_mix, s_inv, s_exps, smalls, full_one = self_kept
    cross_kept = run_steps(
        cross_forward,
        "cross_forward",
        13,
        where,
        (start, s_mix, encoded_before, encoded, encoded_after, hot, cross_bias),
        (smalls,),
        (full_two,),
        (
            tokens(rows, BF16),
            tokens(rows, F32),
            tokens(rows, F32, LANES),
            tokens(rows, BF16),
            tokens(wide, BF16),
            tokens(wide, BF16),
            tokens(rows, F32),
            tokens(rows, F32),
            ((batch, HEADS, rows, wide), BF16),
            tokens(rows, F32),
            tokens(rows, F32),
            tokens(rows, F32, LANES),
        ),
        (((512, 2560), BF16),),
    )
    if stepped:
        near_feed = [up_line, up_near, down_line, down_near]
        near_other = other_core(near_feed)
        cross_kept, up_far, down_far, near_other = tie(cross_kept, up_far, down_far, near_other)
        far_other = other_core([up_far, down_far])
        full_feed = [*near_feed[:2], up_far, *near_feed[2:], down_far]
        full_feed += [*near_other[:2], far_other[0], *near_other[2:], far_other[1]]
    (
        norm_low,
        unit_one,
        scale_one,
        c_q,
        c_k,
        c_v,
        c_mix,
        c_inv,
        c_exps,
        normed_two,
        unit_two,
        scale_two,
        full_two,
    ) = cross_kept
    count = batch * rows
    hidden = 512 * chunks

    def flat(array):
        return array.reshape(count, array.shape[-1])

    vmem = pl.BlockSpec(memory_space=pltpu.VMEM)
    three_specs = grad_specs(block, 2 * hidden)
    feed_scratch = [
        pltpu.VMEM((count, hidden), BF16),
        pltpu.VMEM((count, hidden), F32),
        pltpu.VMEM((512, 2 * hidden), BF16),
    ]
    if len(full_feed) > 1:
        feed_scratch.append(pltpu.VMEM((512, 2 * hidden), BF16))
    output, d_two, feed_sums, *grad_three = pl.pallas_call(
        functools.partial(feed_both, shards, len(full_feed), len(three_specs)),
        in_specs=[pl.BlockSpec(memory_space=pltpu.SMEM)] + [vmem] * (5 + len(full_feed)),
        out_specs=[vmem] * (3 + len(three_specs)),
        out_shape=[
            jax.ShapeDtypeStruct((count, 512), BF16),
            jax.ShapeDtypeStruct((count, 512), F32),
            jax.ShapeDtypeStruct((SMALL_ROWS, 512), F32),
            *(jax.ShapeDtypeStruct(*spec) for spec in three_specs),
        ],
        scratch_shapes=feed_scratch,
        compiler_params=pltpu.CompilerParams(vmem_limit_bytes=29 * MIB),
        cost_estimate=busy(13),
        name="feed_both",
    )(
        where,
        flat(normed_two),
        flat(unit_two),
        flat(scale_two),
        flat(cotangent),
        smalls,
        *full_feed,
    )
    d_two = d_two.reshape(batch, rows, 512)
    cross_heads = run_steps(
        cross_attend_back,
        "cross_attend_back",
        12,
        where,
        (d_two, c_q, c_k, c_v, c_mix, c_inv, c_exps),
        (),
        (),
        (tokens(rows, BF16), tokens(wide, BF16), tokens(wide, BF16)),
        (),
        (),
        ((full_two, 4),),
    )
    if stepped:
        three_got = swapped(grad_three[1], 1)
        cross_heads, three_got = tie(cross_heads, three_got)
        three_parts = add_parts([[grad_three[0], three_got]], 16, "feed_cores")
        cross_heads, three_parts = tie(cross_heads, three_parts)
        three_parts = across_parts(three_parts)
    cross_back = run_steps(
        functools.partial(cross_backward, shards),
        "cross_backward",
        11,
        where,
        (
            d_two,
            c_mix,
            s_mix,
            encoded_before,
            encoded,
            encoded_after,
            norm_low,
            unit_one,
            scale_one,
            *cross_heads,
        ),
        (smalls,),
        ((full_two,),),
        (
            tokens(rows, F32),
            tokens(rows, BF16),
            tokens(MAXLEN, BF16),
            tokens(rows, F32),
            tokens(MAXLEN, BF16),
        ),
        (((SMALL_ROWS, 512), F32), *grad_specs(block, 2560)),
        (pltpu.VMEM((512, 2560), F32),),
    )
    if stepped:
        cross_back, three_parts[1] = tie(cross_back, three_parts[1])
    d_one, d_self_mix, source_before, source_here, source_after, cross_sums, *grad_two = cross_back
    if stepped:
        two_got = swapped(grad_two[1], 1)
    self_back = run_steps(
        functools.partial(self_backward, shards),
        "self_backward",
        15,
        where,
        (d_one, d_self_mix, start_low, hot, tags, s_q, s_k, s_v, s_mix, s_inv, s_exps),
        (feed_sums, cross_sums),
        ((full_one,),),
        (tokens(MAXLEN, BF16), tokens(rows, F32)),
        grad_specs(block, 1536 + LANES),
        (pltpu.VMEM((512, 1536 + LANES), F32), pltpu.VMEM((SMALL_ROWS, 512), F32)),
    )
    if stepped:
        self_back, two_got, three_parts = tie(self_back, two_got, three_parts)
    start_before, start_here, *grad_one = self_back
    columns = 2 * hidden + 4096 + LANES
    if stepped:
        one_got = swapped(grad_one[1], 1)
        parts = add_parts([[grad_two[0], two_got], [grad_one[0], one_got]], 16, "attention_cores")
        parts = across_parts(parts)
        three_parts = add_parts([by_shard(three_parts, shards)], eighth, "feed_chips")
        three_parts = around_parts(three_parts)
        parts, three_parts = tie(parts, three_parts)
        parts = add_parts([by_shard(parts, shards)], eighth, "attention_chips")
        parts, three_parts, source_before, source_after, start_before = tie(
            parts, three_parts, source_before, source_after, start_before
        )
        parts = around_parts(parts)
        both_before = shifted(jnp.concatenate([source_before, start_before], 0), -1)
        source_after = shifted(source_after, 1)
        share = add_parts([three_parts, parts], eighth, "all_shards")[0]
        share, both_before, source_after = tie(share, both_before, source_after)
        source_before, start_before = both_before[:batch], both_before[batch:]
        plane = across(share, chips)
        pieces = plane + other_core(plane)
    else:
        pieces = [reduce_whole(grad) for grad in (*grad_three, *grad_two, *grad_one)]
        source_before, source_after = shifted(source_before, -1), shifted(source_after, 1)
        start_before = shifted(start_before, -1)
    grad_encoded = (source_here + source_before + source_after).astype(BF16)
    grad_inputs = (start_here + start_before).astype(BF16)
    grads = finish(
        where,
        shards,
        block,
        columns,
        pieces,
        ((block, 512),) * 8
        + ((block, hidden), (chunks * block, 512))
        + ((1, block),) * TAG_ROW
        + ((tag_table.shape[0], block),),
    )
    return (
        output.reshape(batch, rows, 512),
        grad_inputs,
        grad_encoded,
        *grads[:10],
        *(part.reshape(block) for part in grads[10:-1]),
        grads[-1],
    )


def solution(mesh):
    rows = P("fsdp", "seq", None)
    by_row = P("fsdp", None)
    vector = P("fsdp")
    tags = P(None, "fsdp")
    return jax.shard_map(
        on_device,
        mesh=mesh,
        in_specs=(rows,) * 3 + (by_row,) * 15 + (vector,) * 6 + (tags,),
        out_specs=(rows,) * 3 + (by_row,) * 10 + (vector,) * 6 + (tags,),
        check_vma=False,
    )
```

```python
import functools

import jax
import jax.numpy as jnp
from jax import lax
from jax.experimental import pallas as pl
from jax.experimental.pallas import tpu as pltpu
from jax.sharding import PartitionSpec as P

HEADS = 8
HEAD_DIM = 64
MAXLEN = 256
LANES = 128
SMALL_ROWS = 32
TAG_ROW = 6
EPSILON = 1e-05
MASKED = -1e30
SCALE = HEAD_DIM ** (-0.5)
BF16 = jnp.bfloat16
F32 = jnp.float32
MIB = 2**20
PER_US = 10**9

NN = (((1,), (0,)), ((), ()))
NT = (((1,), (1,)), ((), ()))
TN = (((0,), (0,)), ((), ()))


def dot(left, right, dims=NN):
    return lax.dot_general(left, right, dims, preferred_element_type=F32)


def lane_ids(rows):
    return lax.broadcasted_iota(jnp.int32, (rows, LANES), 1)


def norm_rows(values_in):
    center = values_in - jnp.mean(values_in, -1, keepdims=True)
    inverse = lax.rsqrt(jnp.mean(center * center, -1, keepdims=True) + EPSILON)
    return center * inverse, inverse


def norm_back(grad_rows, unit_rows, inverse, gain):
    scaled = grad_rows * gain
    centered = (
        scaled
        - jnp.mean(scaled, -1, keepdims=True)
        - unit_rows * jnp.mean(scaled * unit_rows, -1, keepdims=True)
    )
    return inverse * centered


def column_sums(values_in):
    return jnp.sum(values_in, 0, keepdims=True)


def attend(queries, keys, values, query_hot, key_bias, own_bias, exps_ref):
    rows, width = queries.shape[0], keys.shape[0]
    low = lane_ids(rows) < HEAD_DIM
    ones = jnp.ones((width, LANES), BF16)
    mixes, inverses = [], []
    for pair in range(HEADS // 2):
        cols = slice(LANES * pair, LANES * (pair + 1))
        pair_q = queries[:, cols]
        pair_k = jnp.concatenate([keys[:, cols], key_bias], 1)
        pair_v = jnp.concatenate([values[:, cols], ones], 1)
        sums = []
        for half in (0, 1):
            mine = low if half == 0 else ~low
            head_q = jnp.concatenate([jnp.where(mine, pair_q, jnp.zeros_like(pair_q)), query_hot], 1)
            scores = dot(head_q, pair_k, NT)
            if own_bias is not None:
                near = width - rows
                scores = jnp.concatenate([scores[:, :near], scores[:, near:] + own_bias], 1)
            highest = jnp.max(scores, -1, keepdims=True)
            exps = jnp.exp(scores - highest).astype(BF16)
            exps_ref[0, 2 * pair + half] = exps
            sums.append(dot(exps, pair_v))
        inverse = 1.0 / jnp.where(low, sums[0][:, LANES:], sums[1][:, LANES:])
        mixes.append(jnp.where(low, sums[0][:, :LANES], sums[1][:, :LANES]) * inverse)
        inverses.append(inverse)
    return jnp.concatenate(mixes, 1), jnp.concatenate(inverses, 1)


def attend_back(queries, keys, values, exps_ref, mix, inverse, grad_mix):
    rows, width = queries.shape[0], keys.shape[0]
    lane = lane_ids(rows)
    low = lane < HEAD_DIM
    low_wide = lane_ids(width) < HEAD_DIM
    two_ones = jnp.where(lane_ids(width) < 2, 1.0, 0.0).astype(BF16)
    grads_q, grads_k, grads_v = [], [], []
    for pair in range(HEADS // 2):
        cols = slice(LANES * pair, LANES * (pair + 1))
        pair_q, pair_k = queries[:, cols], keys[:, cols]
        pair_v = jnp.concatenate([values[:, cols], two_ones], 1)
        scaled = (grad_mix[:, cols].astype(F32) * inverse[:, cols]).astype(BF16)
        product = scaled.astype(F32) * mix[:, cols]
        found_q, found_k, found_v = [], [], []
        for half in (0, 1):
            mine = low if half == 0 else ~low
            centre = jnp.sum(jnp.where(mine, product, 0.0), -1, keepdims=True)
            coarse = centre.astype(BF16).astype(F32)
            shift = jnp.where(lane == 0, -coarse, jnp.where(lane == 1, coarse - centre, 0.0))
            head_g = jnp.concatenate(
                [jnp.where(mine, scaled, jnp.zeros_like(scaled)), shift.astype(BF16)], 1
            )
            exps = exps_ref[0, 2 * pair + half]
            grad_scores = (exps.astype(F32) * dot(head_g, pair_v, NT)).astype(BF16)
            found_q.append(dot(grad_scores, pair_k))
            found_k.append(dot(grad_scores, pair_q, TN))
            found_v.append(dot(exps, scaled, TN))
        grads_q.append(jnp.where(low, found_q[0], found_q[1]) * SCALE)
        grads_k.append(jnp.where(low_wide, found_k[0], found_k[1]))
        grads_v.append(jnp.where(low_wide, found_v[0], found_v[1]))
    return [jnp.concatenate(part, 1).astype(BF16) for part in (grads_q, grads_k, grads_v)]


def matrix(ref, number, width=512):
    return ref[:, number * width : (number + 1) * width]


def self_forward(
    shards,
    where_ref,
    before_ref,
    here_ref,
    hot_ref,
    tag_ref,
    bias_ref,
    own_ref,
    weight_ref,
    start_ref,
    low_ref,
    q_ref,
    k_ref,
    v_ref,
    mix_ref,
    inv_ref,
    exps_ref,
    small_ref,
    one_ref,
):
    rows = here_ref.shape[1]
    block = 512 // shards

    @pl.when(pl.program_id(0) == 0)
    def _():
        one_ref[...] = weight_ref[...]

    smalls = jnp.concatenate(
        [
            weight_ref[z * block : z * block + SMALL_ROWS, 1536 : 1536 + block]
            for z in range(shards)
        ],
        1,
    )
    small_ref[...] = smalls.astype(F32)
    seg_tags = dot(tag_ref[0], smalls, TN).astype(BF16)
    hot = hot_ref[0, : MAXLEN + rows]
    tokens = jnp.concatenate([before_ref[0], here_ref[0]], 0).astype(F32)
    start = tokens + dot(hot, seg_tags)
    start_ref[0] = start[MAXLEN:]
    start_low = start.astype(BF16)
    low_ref[0] = start_low
    queries = (dot(start_low[MAXLEN:], matrix(weight_ref, 0)).astype(BF16).astype(F32) * SCALE).astype(BF16)
    keys = dot(start_low, matrix(weight_ref, 1)).astype(BF16)
    values = dot(start_low, matrix(weight_ref, 2)).astype(BF16)
    q_ref[0] = queries
    k_ref[0] = keys
    v_ref[0] = values
    mix_ref[0], inv_ref[0] = attend(
        queries, keys, values, hot[MAXLEN:], bias_ref[0], own_ref[0], exps_ref
    )


def cross_forward(
    where_ref,
    start_ref,
    self_mix_ref,
    before_ref,
    here_ref,
    after_ref,
    hot_ref,
    bias_ref,
    small_ref,
    weight_ref,
    norm_low_ref,
    unit_one_ref,
    scale_one_ref,
    q_ref,
    k_ref,
    v_ref,
    mix_ref,
    inv_ref,
    exps_ref,
    normed_ref,
    unit_two_ref,
    scale_two_ref,
    two_ref,
):
    rows = start_ref.shape[1]

    @pl.when(pl.program_id(0) == 0)
    def _():
        two_ref[...] = weight_ref[...]

    source = jnp.concatenate([before_ref[0], here_ref[0], after_ref[0]], 0)
    keys = dot(source, matrix(weight_ref, 2)).astype(BF16)
    values = dot(source, matrix(weight_ref, 3)).astype(BF16)
    k_ref[0] = keys
    v_ref[0] = values
    branch = dot(self_mix_ref[0].astype(BF16), matrix(weight_ref, 0))
    unit_one, scale_one = norm_rows(start_ref[0] + branch)
    unit_one_ref[0] = unit_one
    scale_one_ref[0] = jnp.broadcast_to(scale_one, (rows, LANES))
    normed_one = unit_one * small_ref[0:1] + small_ref[1:2]
    norm_low = normed_one.astype(BF16)
    norm_low_ref[0] = norm_low
    queries = (dot(norm_low, matrix(weight_ref, 1)).astype(BF16).astype(F32) * SCALE).astype(BF16)
    q_ref[0] = queries
    mix, inverse = attend(
        queries, keys, values, hot_ref[0, MAXLEN : MAXLEN + rows], bias_ref[0], None, exps_ref
    )
    mix_ref[0] = mix
    inv_ref[0] = inverse
    branch = dot(mix.astype(BF16), matrix(weight_ref, 4))
    unit_two, scale_two = norm_rows(normed_one + branch)
    unit_two_ref[0] = unit_two
    scale_two_ref[0] = jnp.broadcast_to(scale_two, (rows, LANES))
    normed_ref[0] = unit_two * small_ref[2:3] + small_ref[3:4]


GELU_A = 0.7978845608028654
GELU_B = 0.044715


def feed_both(
    shards,
    pieces,
    grads,
    where_ref,
    normed_ref,
    unit_ref,
    scale_ref,
    cotangent_ref,
    small_ref,
    *rest,
):
    piece_refs, rest = rest[:pieces], rest[pieces:]
    out_ref, back_ref, sums_ref, *rest = rest
    grad_refs, rest = rest[:grads], rest[grads:]
    act_ref, slope_ref, grad_ref, *rest = rest
    weight_ref = piece_refs[0]
    if pieces > 1:
        (weight_ref,) = rest
        assemble(where_ref, piece_refs, weight_ref)
    normed = normed_ref[...]
    normed_low = normed.astype(BF16)
    chunks = weight_ref.shape[1] // 1024
    feed = normed
    for part in range(chunks):
        cols = slice(512 * part, 512 * (part + 1))
        hidden = dot(normed_low, matrix(weight_ref, part))
        square = hidden * hidden
        bend = jnp.tanh(hidden * (GELU_A + GELU_A * GELU_B * square))
        rise = 0.5 + 0.5 * bend
        act = (hidden * rise).astype(BF16)
        act_ref[:, cols] = act
        slope_ref[:, cols] = rise + rise * (1.0 - bend) * hidden * (
            GELU_A + 3.0 * GELU_A * GELU_B * square
        )
        feed = feed + dot(act, matrix(weight_ref, chunks + part))
    unit, scale = norm_rows(feed)
    gain = small_ref[4:5]
    out_ref[...] = (unit * gain + small_ref[5:6]).astype(BF16)
    grad = cotangent_ref[...].astype(F32)
    sums_ref[...] = jnp.zeros_like(sums_ref)
    sums_ref[4:5] = column_sums(grad * unit)
    sums_ref[5:6] = column_sums(grad)
    d_three = norm_back(grad, unit, scale, gain)
    d_feed = d_three.astype(BF16)
    total = d_three
    for part in range(chunks):
        cols = slice(512 * part, 512 * (part + 1))
        late = slice(512 * (chunks + part), 512 * (chunks + part + 1))
        grad_ref[:, late] = dot(act_ref[:, cols], d_feed, TN).astype(BF16)
        d_hidden = (
            slope_ref[:, cols] * dot(d_feed, matrix(weight_ref, chunks + part), NT)
        ).astype(BF16)
        grad_ref[:, cols] = dot(normed_low, d_hidden, TN).astype(BF16)
        total = total + dot(d_hidden, matrix(weight_ref, part), NT)
    unit_two = unit_ref[...]
    sums_ref[2:3] = column_sums(total * unit_two)
    sums_ref[3:4] = column_sums(total)
    back_ref[...] = norm_back(total, unit_two, scale_ref[:, 0:1], small_ref[2:3])
    give(shards, where_ref, grad_ref, grad_refs)


def cross_attend_back(
    where_ref,
    back_ref,
    q_ref,
    k_ref,
    v_ref,
    mix_ref,
    inv_ref,
    exps_ref,
    weight_ref,
    d_q_ref,
    d_k_ref,
    d_v_ref,
):
    d_mix = dot(back_ref[0].astype(BF16), weight_ref[...], NT).astype(BF16)
    d_q_ref[0], d_k_ref[0], d_v_ref[0] = attend_back(
        q_ref[0], k_ref[0], v_ref[0], exps_ref, mix_ref[0], inv_ref[0], d_mix
    )


def add_columns(total_ref, number, value):
    cols = slice(512 * number, 512 * (number + 1))
    total_ref[:, cols] = total_ref[:, cols] + value


def cross_backward(
    shards,
    where_ref,
    back_ref,
    mix_ref,
    self_mix_ref,
    before_ref,
    here_ref,
    after_ref,
    norm_low_ref,
    unit_ref,
    scale_ref,
    d_q_ref,
    d_k_ref,
    d_v_ref,
    small_ref,
    weight_ref,
    one_ref,
    d_mix_ref,
    source_before_ref,
    source_here_ref,
    source_after_ref,
    sums_ref,
    *rest,
):
    *grad_refs, total_ref = rest
    step = pl.program_id(0)
    rows = here_ref.shape[1]

    @pl.when(step == 0)
    def _():
        total_ref[...] = jnp.zeros_like(total_ref)
        sums_ref[...] = jnp.zeros_like(sums_ref)

    d_two = back_ref[0]
    d_q, d_k, d_v = d_q_ref[0], d_k_ref[0], d_v_ref[0]
    add_columns(total_ref, 4, dot(mix_ref[0].astype(BF16), d_two.astype(BF16), TN))
    source = jnp.concatenate([before_ref[0], here_ref[0], after_ref[0]], 0)
    add_columns(total_ref, 2, dot(source, d_k, TN))
    add_columns(total_ref, 3, dot(source, d_v, TN))
    d_source = dot(d_k, matrix(weight_ref, 2), NT) + dot(d_v, matrix(weight_ref, 3), NT)
    source_before_ref[0] = d_source[:MAXLEN].astype(BF16)
    source_here_ref[0] = d_source[MAXLEN : MAXLEN + rows]
    source_after_ref[0] = d_source[MAXLEN + rows :].astype(BF16)
    add_columns(total_ref, 1, dot(norm_low_ref[0], d_q, TN))
    total = d_two + dot(d_q, matrix(weight_ref, 1), NT)
    unit = unit_ref[0]
    sums_ref[0:1] = sums_ref[0:1] + column_sums(total * unit)
    sums_ref[1:2] = sums_ref[1:2] + column_sums(total)
    d_one = norm_back(total, unit, scale_ref[0, :, 0:1], small_ref[0:1])
    one_ref[0] = d_one
    d_one_low = d_one.astype(BF16)
    add_columns(total_ref, 0, dot(self_mix_ref[0].astype(BF16), d_one_low, TN))
    d_mix_ref[0] = dot(d_one_low, matrix(weight_ref, 0), NT).astype(BF16)

    @pl.when(step == pl.num_programs(0) - 1)
    def _():
        give(shards, where_ref, total_ref, grad_refs)


def self_backward(
    shards,
    where_ref,
    one_ref,
    d_mix_ref,
    low_ref,
    hot_ref,
    tag_ref,
    q_ref,
    k_ref,
    v_ref,
    mix_ref,
    inv_ref,
    exps_ref,
    feed_sums_ref,
    cross_sums_ref,
    weight_ref,
    before_ref,
    here_ref,
    *rest,
):
    *grad_refs, total_ref, sums_ref = rest
    step = pl.program_id(0)
    rows = one_ref.shape[1]

    @pl.when(step == 0)
    def _():
        total_ref[...] = jnp.zeros_like(total_ref)
        sums_ref[...] = feed_sums_ref[...] + cross_sums_ref[...]

    def add(number, value):
        cols = slice(512 * number, 512 * (number + 1))
        total_ref[:, cols] = total_ref[:, cols] + value

    d_one = one_ref[0]
    d_mix = d_mix_ref[0]
    d_q, d_k, d_v = attend_back(
        q_ref[0], k_ref[0], v_ref[0], exps_ref, mix_ref[0], inv_ref[0], d_mix
    )
    start_low = low_ref[0]
    add(0, dot(start_low[MAXLEN:], d_q, TN))
    add(1, dot(start_low, d_k, TN))
    add(2, dot(start_low, d_v, TN))
    d_start = dot(d_k, matrix(weight_ref, 1), NT) + dot(d_v, matrix(weight_ref, 2), NT)
    d_before = d_start[:MAXLEN].astype(BF16)
    d_here = d_start[MAXLEN:] + d_one + dot(d_q, matrix(weight_ref, 0), NT)
    before_ref[0] = d_before
    here_ref[0] = d_here
    both = jnp.concatenate([d_before, d_here.astype(BF16)], 0)
    seg_sums = dot(hot_ref[0, : MAXLEN + rows], both, TN)
    coarse = seg_sums.astype(BF16)
    fine = (seg_sums - coarse.astype(F32)).astype(BF16)
    sums_ref[...] = sums_ref[...] + dot(tag_ref[0], coarse) + dot(tag_ref[0], fine)

    @pl.when(step == pl.num_programs(0) - 1)
    def _():
        block = 512 // shards
        for z in range(shards):
            total_ref[z * block : z * block + SMALL_ROWS, 1536 : 1536 + block] = sums_ref[
                :, z * block : (z + 1) * block
            ]
        give(shards, where_ref, total_ref, grad_refs)


def busy(micros):
    return pl.CostEstimate(
        flops=micros * PER_US, bytes_accessed=micros * 2 * MIB, transcendentals=0
    )


def per_step(array, first=0):
    rest = (0,) * (array.ndim - 1)
    return pl.BlockSpec((1,) + array.shape[1:], lambda step: (first + step,) + rest)


def whole(array):
    rest = (0,) * array.ndim
    return pl.BlockSpec(array.shape, lambda step: rest)


def run_steps(
    body,
    name,
    micros,
    where,
    stepped,
    fixed,
    weights,
    stepped_outs,
    fixed_outs,
    scratch=(),
    squares=(),
    first=0,
    last=None,
    previous=(),
):
    batch = stepped[0].shape[0]
    last = batch if last is None else last
    outs = [jax.ShapeDtypeStruct(*spec) for spec in (*stepped_outs, *fixed_outs)]
    counts = [len(stepped), len(fixed), *(len(pieces) for pieces in weights)]
    outs_count = len(outs)
    whole_scratch = [
        pltpu.VMEM((512, pieces[0].shape[-1]), BF16) for pieces in weights if len(pieces) > 1
    ]

    def called(where_ref, *refs):
        refs = list(refs)

        def take(count):
            taken = refs[:count]
            del refs[:count]
            return taken

        plain = take(counts[0] + counts[1])
        pieces = [take(count) for count in counts[2:]]
        square_refs = take(len(squares))
        take(len(previous))
        outs_refs = take(outs_count)
        own_scratch = take(len(scratch))
        fulls = []
        for piece_refs in pieces:
            if len(piece_refs) == 1:
                fulls.append(piece_refs[0])
                continue
            (full_ref,) = take(1)
            fulls.append(full_ref)

            @pl.when(pl.program_id(0) == 0)
            def _(piece_refs=piece_refs, full_ref=full_ref):
                assemble(where_ref, piece_refs, full_ref)

        body(where_ref, *plain, *fulls, *square_refs, *outs_refs, *own_scratch)

    flat_weights = [piece for pieces in weights for piece in pieces]
    steps = len(stepped_outs)
    return pl.pallas_call(
        called,
        grid=(last - first,),
        in_specs=[pl.BlockSpec(memory_space=pltpu.SMEM)]
        + [per_step(a, first) for a in stepped]
        + [whole(a) for a in (*fixed, *flat_weights)]
        + [pl.BlockSpec((512, 512), lambda step, number=number: (0, number)) for _, number in squares]
        + [pl.BlockSpec(memory_space=pl.ANY)] * len(previous),
        out_specs=[per_step(a, first) for a in outs[:steps]] + [whole(a) for a in outs[steps:]],
        out_shape=outs,
        scratch_shapes=[*scratch, *whole_scratch],
        compiler_params=pltpu.CompilerParams(vmem_limit_bytes=20 * MIB),
        input_output_aliases={
            1 + len(stepped) + len(fixed) + len(flat_weights) + len(squares) + number: number
            for number in range(len(previous))
        },
        cost_estimate=busy(micros),
        name=name,
    )(where, *stepped, *fixed, *flat_weights, *(array for array, _ in squares), *previous)


def grad_specs(block, columns):
    if not by_shares(block):
        return (((512, columns), BF16),)
    places = lax.axis_size("seq")
    return (((places // 2, 512 // places, columns), BF16),) * 2


def give(shards, where_ref, total_ref, refs):
    if len(refs) == 1:
        refs[0][...] = total_ref[...].astype(BF16)
    else:
        split_shares(shards, where_ref, total_ref, *refs)


def pack_body(chunks, shards, place_ref, *refs):
    ins, (low_ref, small_ref) = refs[:-2], refs[-2:]
    squares, (up_ref, down_ref, tag_ref), vectors = ins[:8], ins[8:11], ins[11:]
    eighth = low_ref.shape[0]
    block = small_ref.shape[0]
    small_ref[...] = jnp.zeros_like(small_ref)
    for row, vector_ref in enumerate(vectors):
        small_ref[row : row + 1, :block] = vector_ref[...].astype(F32)
    small_ref[TAG_ROW : TAG_ROW + tag_ref.shape[0], :block] = tag_ref[...].astype(F32)
    for number in range(3):
        low_ref[:, 512 * number : 512 * (number + 1)] = squares[number][...]
    row = pl.multiple_of(place_ref[0] * eighth, eighth)
    low_ref[:, 1536 : 1536 + LANES] = small_ref[pl.ds(row, eighth), :].astype(BF16)
    for number in range(5):
        lane = 1536 + LANES + 512 * number
        low_ref[:, lane : lane + 512] = squares[3 + number][...]
    for part in range(chunks):
        for shard in range(shards):
            here = (shard * chunks + part) * block
            there = 4096 + LANES + part * 512 + shard * block
            low_ref[:, there : there + block] = up_ref[:, here : here + block]
        lane = 4096 + LANES + 512 * (chunks + part)
        low_ref[:, lane : lane + 512] = down_ref[part]


def pack_shares(places, chunks, shards, squares, up, down, tags, vectors):
    block = squares[0].shape[0]
    eighth = block // 8
    columns = 4096 + LANES + 2 * up.shape[1]

    def rows_at(step, place):
        return place[0], 0

    return pl.pallas_call(
        functools.partial(pack_body, chunks, shards),
        grid_spec=pltpu.PrefetchScalarGridSpec(
            num_scalar_prefetch=1,
            grid=(1,),
            in_specs=[pl.BlockSpec((eighth, 512), rows_at)] * 8
            + [
                pl.BlockSpec((eighth, up.shape[1]), rows_at),
                pl.BlockSpec((chunks, eighth, 512), lambda step, place: (0, place[0], 0)),
                pl.BlockSpec(tags.shape, lambda step, place: (0, 0)),
            ]
            + [pl.BlockSpec((1, block), lambda step, place: (0, 0))] * len(vectors),
            out_specs=pl.BlockSpec((eighth, columns), lambda step, place: (0, 0)),
            scratch_shapes=[pltpu.VMEM((block, LANES), F32)],
        ),
        out_shape=jax.ShapeDtypeStruct((eighth, columns), BF16),
        compiler_params=pltpu.CompilerParams(vmem_limit_bytes=60 * MIB),
        name="pack_shares",
    )(places, *squares, up, down, tags, *(vector[None] for vector in vectors))


def tie(*values):
    return lax.optimization_barrier(values)


def standing():
    place = lax.axis_index("seq")
    return jnp.stack([lax.axis_index("fsdp"), place // 2, place % 2]).astype(jnp.int32)


def swapped(array, mask):
    size = lax.axis_size("seq")
    return lax.ppermute(array, "seq", [(i, i ^ mask) for i in range(size)])


def turned(array, by):
    size = lax.axis_size("fsdp")
    return lax.ppermute(array, "fsdp", [(i, (i + by) % size) for i in range(size)])


def around(share):
    return [share] + [turned(share, k) for k in range(1, lax.axis_size("fsdp"))]


def across(array, chips):
    return [array] + [swapped(array, 2 * m) for m in range(1, chips)]


def other_core(arrays):
    return [swapped(array, 1) for array in arrays]


def across_parts(parts):
    return [parts[0]] + [swapped(parts[m], 2 * m) for m in range(1, len(parts))]


def around_parts(parts):
    return [parts[0][None]] + [turned(parts[k], k)[None] for k in range(1, len(parts))]


def by_shard(arrays, shards):
    return [array.reshape(shards, -1, array.shape[-1]) for array in arrays]


def by_shares(block):
    return lax.axis_size("seq") == 8 and lax.axis_size("fsdp") == 4 and block % 128 == 0


def eighth_row(chip, core, m, t):
    return (chip ^ m) * 2 + (core ^ t)


PLAIN_PIECES = ((0, 0), (1, 0), (2, 0), (3, 0))
FEED_PIECES = ((0, 0), (1, 0), (2, 0), (3, 0), (0, 1), (2, 1), (1, 1), (3, 1))


def assemble(where_ref, piece_refs, full_ref):
    pieces = []
    for ref in piece_refs:
        pieces += [ref] if len(ref.shape) == 3 else [ref.at[i] for i in range(ref.shape[0])]
    shards, rows, columns = pieces[0].shape
    block = full_ref.shape[0] // shards
    places = FEED_PIECES if columns < full_ref.shape[1] else PLAIN_PIECES
    for number, piece_ref in enumerate(pieces):
        t, index = divmod(number, len(places))
        m, half = places[index]
        place = eighth_row(where_ref[1], where_ref[2], m, t)
        for k in range(shards):
            shard = lax.rem(where_ref[0] + shards - k, shards)
            row = pl.multiple_of(shard * block + place * rows, rows)
            full_ref[pl.ds(row, rows), half * columns : (half + 1) * columns] = piece_ref[k]


def split_shares(shards, where_ref, total_ref, keep_ref, send_ref):
    chips, height, _ = keep_ref.shape
    rows = total_ref.shape[0] // (2 * chips * shards)
    block = 2 * chips * rows
    for t, out_ref in enumerate((keep_ref, send_ref)):
        for m in range(chips):
            place = eighth_row(where_ref[1], where_ref[2], m, t)
            for k in range(shards):
                shard = lax.rem(where_ref[0] + k, shards)
                row = pl.multiple_of(shard * block + place * rows, rows)
                out_ref[m, k * rows : (k + 1) * rows, :] = total_ref[pl.ds(row, rows), :].astype(
                    BF16
                )


def add_parts_body(sizes, stacked, *refs):
    ins, outs = refs[: sum(sizes)], refs[sum(sizes) :]
    for number, out_ref in enumerate(outs):
        first, lane = 0, 0
        for size in sizes:
            total = None
            for ref in ins[first : first + size]:
                value = (ref[number] if stacked else ref[...]).astype(F32)
                total = value if total is None else total + value
            columns = total.shape[1]
            out_ref[:, lane : lane + columns] = total.astype(BF16)
            first, lane = first + size, lane + columns


def add_parts(groups, tile, name):
    arrays = [array for group in groups for array in group]
    parts, rows = arrays[0].shape[:2]
    columns = sum(group[0].shape[2] for group in groups)
    return pl.pallas_call(
        functools.partial(add_parts_body, [len(group) for group in groups], True),
        grid=(rows // tile,),
        in_specs=[
            pl.BlockSpec((parts, tile, array.shape[2]), lambda i: (0, i, 0)) for array in arrays
        ],
        out_specs=[pl.BlockSpec((tile, columns), lambda i: (i, 0))] * parts,
        out_shape=[jax.ShapeDtypeStruct((rows, columns), BF16)] * parts,
        compiler_params=pltpu.CompilerParams(vmem_limit_bytes=20 * MIB),
        name=name,
    )(*arrays)


def reduce_whole(grad):
    return lax.psum(lax.psum_scatter(grad, "fsdp", scatter_dimension=0, tiled=True), "seq")


def collect(where_ref, refs, full_ref):
    if full_ref.shape[0] == refs[0].shape[0]:
        lane = 0
        for ref in refs:
            columns = ref.shape[1]
            full_ref[:, lane : lane + columns] = ref[...].astype(F32)
            lane += columns
        return
    half = len(refs) // 2
    rows = refs[0].shape[0]
    for number, ref in enumerate(refs):
        t, m = divmod(number, half)
        row = eighth_row(where_ref[1], where_ref[2], m, t) * rows
        full_ref[pl.ds(pl.multiple_of(row, rows), rows), :] = ref[...].astype(F32)


def finish_body(shards, count, where_ref, *refs):
    ins, outs, full_ref = refs[:count], list(refs[count:-1]), refs[-1]
    collect(where_ref, ins, full_ref)
    block = full_ref.shape[0]
    squares, (up_ref, down_ref), vectors, tag_ref = outs[:8], outs[8:10], outs[10:-1], outs[-1]
    chunks = down_ref.shape[0] // block
    for part in range(chunks):
        for shard in range(shards):
            here = part * 512 + shard * block
            there = (shard * chunks + part) * block
            up_ref[:, there : there + block] = full_ref[:, here : here + block]
        late = 512 * (chunks + part)
        down_ref[part * block : (part + 1) * block, :] = full_ref[:, late : late + 512]
    cross = 1024 * chunks
    late = cross + 5 * 512
    for number in range(8):
        lane = late + 512 * number if number < 3 else cross + 512 * (number - 3)
        squares[number][...] = full_ref[:, lane : lane + 512]
    lane = late + 3 * 512
    for row, vector_ref in enumerate(vectors):
        vector_ref[...] = full_ref[row : row + 1, lane : lane + block]
    tag_ref[...] = full_ref[TAG_ROW : TAG_ROW + tag_ref.shape[0], lane : lane + block]


def finish(where, shards, block, columns, pieces, shapes):
    vmem = pl.BlockSpec(memory_space=pltpu.VMEM)
    return pl.pallas_call(
        functools.partial(finish_body, shards, len(pieces)),
        in_specs=[pl.BlockSpec(memory_space=pltpu.SMEM)] + [vmem] * len(pieces),
        out_specs=[vmem] * len(shapes),
        out_shape=[jax.ShapeDtypeStruct(shape, F32) for shape in shapes],
        scratch_shapes=[pltpu.VMEM((block, columns), F32)],
        compiler_params=pltpu.CompilerParams(vmem_limit_bytes=20 * MIB),
        name="finish",
    )(where, *pieces)


def local_facts(seg_ids, keep_mask, pair_tags, cut_lo, cut_hi, base, rows):
    sentences = pair_tags.shape[1]
    ids = jnp.arange(sentences, dtype=jnp.int32)
    starts = jnp.sum(seg_ids[:, :, None] < ids, 1, dtype=jnp.int32)
    ends = jnp.sum(seg_ids[:, :, None] <= ids, 1, dtype=jnp.int32)
    half = (ends - starts - 1) // 2
    spare = ((0, 0), (0, LANES - sentences))
    lower = jnp.pad(starts + jnp.minimum(cut_lo, half), spare)
    upper = jnp.pad(ends - jnp.minimum(cut_hi, half), spare)
    edge = ((0, 0), (MAXLEN, MAXLEN))
    width = rows + 2 * MAXLEN
    seg = lax.dynamic_slice_in_dim(jnp.pad(seg_ids, edge, constant_values=-1), base, width, 1)
    keep = lax.dynamic_slice_in_dim(jnp.pad(keep_mask, edge), base, width, 1)
    lanes = jnp.arange(LANES, dtype=jnp.int32)
    hot = seg[:, :, None] == lanes
    place = base - MAXLEN + jnp.arange(width, dtype=jnp.int32)[None, :, None]
    inside = (place >= lower[:, None, :]) & (place < upper[:, None, :])
    near = MAXLEN + rows
    seen = (keep[:, :near] == 1) | (jnp.arange(near) >= MAXLEN)
    self_bias = jnp.where(hot[:, :near] & seen[:, :, None], 0.0, MASKED).astype(BF16)
    cross_bias = jnp.where(inside, 0.0, MASKED).astype(BF16)
    spot = jnp.arange(rows, dtype=jnp.int32)
    earlier = (spot[None, :] < spot[:, None]) & (keep[:, None, MAXLEN:near] == 1)
    own_bias = jnp.where(earlier | (spot[None, :] == spot[:, None]), 0.0, MASKED).astype(F32)
    tag_rows = TAG_ROW + pair_tags
    tags = (tag_rows[:, None, :] == jnp.arange(SMALL_ROWS, dtype=jnp.int32)[:, None]).astype(BF16)
    tags = jnp.pad(tags, ((0, 0), (0, 0), (0, LANES - sentences)))
    return hot.astype(BF16), self_bias, cross_bias, own_bias, tags


def shifted(shard, by):
    size = lax.axis_size("seq")
    pairs = [(i, i + by) for i in range(size) if 0 <= i + by < size]
    return lax.ppermute(shard, "seq", pairs)


def on_device(
    inputs,
    encoded,
    cotangent,
    seg_ids,
    keep_mask,
    pair_tags,
    cut_lo,
    cut_hi,
    w_query,
    w_key,
    w_value,
    w_out,
    c_query,
    c_key,
    c_value,
    c_out,
    w_up,
    w_down,
    gain_one,
    bias_one,
    gain_two,
    bias_two,
    gain_three,
    bias_three,
    tag_table,
):
    batch, rows, _ = inputs.shape
    shards = lax.axis_size("fsdp")
    block = w_query.shape[0]
    chunks = w_down.shape[0] // block
    base = lax.axis_index("seq") * rows
    stepped = by_shares(block)
    places = lax.axis_size("seq")
    chips = places // 2
    where = standing()
    both_before = shifted(jnp.concatenate([inputs, encoded], 0), 1)
    encoded_after = shifted(encoded, -1)

    down_blocks = w_down.reshape(chunks, block, 512)
    vectors = (gain_one, bias_one, gain_two, bias_two, gain_three, bias_three)
    squares = (w_query, w_key, w_value, w_out, c_query, c_key, c_value, c_out)
    eighth = block // places
    if stepped:
        place = lax.axis_index("seq").astype(jnp.int32)[None]
        share = pack_shares(
            place, chunks, shards, squares, w_up, down_blocks, tag_table, vectors
        )
        line = around(share)
        bounds = (0, 1536 + LANES, 4096 + LANES, 4096 + LANES + 512 * chunks, share.shape[1])
        line_one, line_two, up_line, down_line = [
            jnp.stack([part[:, first:last] for part in line])
            for first, last in zip(bounds[:-1], bounds[1:])
        ]
        line_one, line_two, up_line, down_line, seg_ids, keep_mask, both_before, encoded_after = tie(
            line_one, line_two, up_line, down_line, seg_ids, keep_mask, both_before, encoded_after
        )
        plane_one = across(line_one, chips)
        plane_one, line_two, up_line, down_line = tie(plane_one, line_two, up_line, down_line)
        full_one = plane_one + other_core(plane_one)
        plane_two = across(line_two, chips)
        up_near, down_near = swapped(up_line, 2), swapped(down_line, 4)
    else:
        small = jnp.concatenate([jnp.stack(vectors), tag_table], 0)
        small = jnp.pad(small, ((0, block - small.shape[0]), (0, LANES - small.shape[1])))
        up = w_up.reshape(block, shards, chunks, block).swapaxes(1, 2).reshape(block, -1)
        down = down_blocks.swapaxes(0, 1).reshape(block, -1)
        full_one, full_two, full_feed = [
            [lax.all_gather(jnp.concatenate(pack, 1), "fsdp", axis=0, tiled=True)]
            for pack in ((*squares[:3], small), squares[3:], (up, down))
        ]

    inputs_before, encoded_before = both_before[:batch], both_before[batch:]
    hot, self_bias, cross_bias, own_bias, tags = local_facts(
        seg_ids, keep_mask, pair_tags, cut_lo, cut_hi, base, rows
    )
    near, wide = MAXLEN + rows, 2 * MAXLEN + rows

    def tokens(count, kind, width=512):
        return ((batch, count, width), kind)

    self_kept = run_steps(
        functools.partial(self_forward, shards),
        "self_forward",
        8,
        where,
        (inputs_before, inputs, hot, tags, self_bias, own_bias),
        (),
        (full_one,),
        (
            tokens(rows, F32),
            tokens(near, BF16),
            tokens(rows, BF16),
            tokens(near, BF16),
            tokens(near, BF16),
            tokens(rows, F32),
            tokens(rows, F32),
            ((batch, HEADS, rows, near), BF16),
        ),
        (((SMALL_ROWS, 512), F32), ((512, 1536 + LANES), BF16)),
    )
    if stepped:
        self_kept, plane_two = tie(self_kept, plane_two)
        full_two = plane_two + other_core(plane_two)
        full_two, up_near, down_near = tie(full_two, up_near, down_near)
        up_far = swapped(jnp.stack([up_line, up_near]), 4)
        down_far = swapped(jnp.stack([down_line, down_near]), 2)
    start, start_low, s_q, s_k, s_v, s_mix, s_inv, s_exps, smalls, full_one = self_kept
    cross_kept = run_steps(
        cross_forward,
        "cross_forward",
        13,
        where,
        (start, s_mix, encoded_before, encoded, encoded_after, hot, cross_bias),
        (smalls,),
        (full_two,),
        (
            tokens(rows, BF16),
            tokens(rows, F32),
            tokens(rows, F32, LANES),
            tokens(rows, BF16),
            tokens(wide, BF16),
            tokens(wide, BF16),
            tokens(rows, F32),
            tokens(rows, F32),
            ((batch, HEADS, rows, wide), BF16),
            tokens(rows, F32),
            tokens(rows, F32),
            tokens(rows, F32, LANES),
        ),
        (((512, 2560), BF16),),
    )
    if stepped:
        near_feed = [up_line, up_near, down_line, down_near]
        near_other = other_core(near_feed)
        cross_kept, up_far, down_far, near_other = tie(cross_kept, up_far, down_far, near_other)
        far_other = other_core([up_far, down_far])
        full_feed = [*near_feed[:2], up_far, *near_feed[2:], down_far]
        full_feed += [*near_other[:2], far_other[0], *near_other[2:], far_other[1]]
    (
        norm_low,
        unit_one,
        scale_one,
        c_q,
        c_k,
        c_v,
        c_mix,
        c_inv,
        c_exps,
        normed_two,
        unit_two,
        scale_two,
        full_two,
    ) = cross_kept
    count = batch * rows
    hidden = 512 * chunks

    def flat(array):
        return array.reshape(count, array.shape[-1])

    vmem = pl.BlockSpec(memory_space=pltpu.VMEM)
    three_specs = grad_specs(block, 2 * hidden)
    feed_scratch = [
        pltpu.VMEM((count, hidden), BF16),
        pltpu.VMEM((count, hidden), F32),
        pltpu.VMEM((512, 2 * hidden), BF16),
    ]
    if len(full_feed) > 1:
        feed_scratch.append(pltpu.VMEM((512, 2 * hidden), BF16))
    output, d_two, feed_sums, *grad_three = pl.pallas_call(
        functools.partial(feed_both, shards, len(full_feed), len(three_specs)),
        in_specs=[pl.BlockSpec(memory_space=pltpu.SMEM)] + [vmem] * (5 + len(full_feed)),
        out_specs=[vmem] * (3 + len(three_specs)),
        out_shape=[
            jax.ShapeDtypeStruct((count, 512), BF16),
            jax.ShapeDtypeStruct((count, 512), F32),
            jax.ShapeDtypeStruct((SMALL_ROWS, 512), F32),
            *(jax.ShapeDtypeStruct(*spec) for spec in three_specs),
        ],
        scratch_shapes=feed_scratch,
        compiler_params=pltpu.CompilerParams(vmem_limit_bytes=29 * MIB),
        cost_estimate=busy(13),
        name="feed_both",
    )(
        where,
        flat(normed_two),
        flat(unit_two),
        flat(scale_two),
        flat(cotangent),
        smalls,
        *full_feed,
    )
    d_two = d_two.reshape(batch, rows, 512)
    head_args = (
        where,
        (d_two, c_q, c_k, c_v, c_mix, c_inv, c_exps),
        (),
        (),
        (tokens(rows, BF16), tokens(wide, BF16), tokens(wide, BF16)),
        (),
        (),
        ((full_two, 4),),
    )
    cut = batch // 2 if stepped else batch
    cross_heads = run_steps(cross_attend_back, "cross_attend_back", 5, *head_args, last=cut)
    if stepped:
        three_got = swapped(grad_three[1], 1)
        cross_heads, three_got = tie(cross_heads, three_got)
        three_parts = add_parts([[grad_three[0], three_got]], 16, "feed_cores")
        cross_heads, three_parts = tie(cross_heads, three_parts)
        three_parts = across_parts(three_parts)
        cross_heads = run_steps(
            cross_attend_back,
            "cross_attend_rest",
            5,
            *head_args,
            first=cut,
            previous=cross_heads,
        )
    cross_back = run_steps(
        functools.partial(cross_backward, shards),
        "cross_backward",
        11,
        where,
        (
            d_two,
            c_mix,
            s_mix,
            encoded_before,
            encoded,
            encoded_after,
            norm_low,
            unit_one,
            scale_one,
            *cross_heads,
        ),
        (smalls,),
        ((full_two,),),
        (
            tokens(rows, F32),
            tokens(rows, BF16),
            tokens(MAXLEN, BF16),
            tokens(rows, F32),
            tokens(MAXLEN, BF16),
        ),
        (((SMALL_ROWS, 512), F32), *grad_specs(block, 2560)),
        (pltpu.VMEM((512, 2560), F32),),
    )
    if stepped:
        cross_back, three_parts[1] = tie(cross_back, three_parts[1])
    d_one, d_self_mix, source_before, source_here, source_after, cross_sums, *grad_two = cross_back
    if stepped:
        two_got = swapped(grad_two[1], 1)
    self_back = run_steps(
        functools.partial(self_backward, shards),
        "self_backward",
        15,
        where,
        (d_one, d_self_mix, start_low, hot, tags, s_q, s_k, s_v, s_mix, s_inv, s_exps),
        (feed_sums, cross_sums),
        ((full_one,),),
        (tokens(MAXLEN, BF16), tokens(rows, F32)),
        grad_specs(block, 1536 + LANES),
        (pltpu.VMEM((512, 1536 + LANES), F32), pltpu.VMEM((SMALL_ROWS, 512), F32)),
    )
    if stepped:
        self_back, two_got, three_parts = tie(self_back, two_got, three_parts)
    start_before, start_here, *grad_one = self_back
    columns = 2 * hidden + 4096 + LANES
    if stepped:
        one_got = swapped(grad_one[1], 1)
        parts = add_parts([[grad_two[0], two_got], [grad_one[0], one_got]], 16, "attention_cores")
        parts = across_parts(parts)
        three_parts = add_parts([by_shard(three_parts, shards)], eighth, "feed_chips")
        three_parts = around_parts(three_parts)
        parts, three_parts = tie(parts, three_parts)
        parts = add_parts([by_shard(parts, shards)], eighth, "attention_chips")
        parts, three_parts, source_before, source_after, start_before = tie(
            parts, three_parts, source_before, source_after, start_before
        )
        parts = around_parts(parts)
        both_before = shifted(jnp.concatenate([source_before, start_before], 0), -1)
        source_after = shifted(source_after, 1)
        share = add_parts([three_parts, parts], eighth, "all_shards")[0]
        share, both_before, source_after = tie(share, both_before, source_after)
        source_before, start_before = both_before[:batch], both_before[batch:]
        plane = across(share, chips)
        pieces = plane + other_core(plane)
    else:
        pieces = [reduce_whole(grad) for grad in (*grad_three, *grad_two, *grad_one)]
        source_before, source_after = shifted(source_before, -1), shifted(source_after, 1)
        start_before = shifted(start_before, -1)
    grad_encoded = (source_here + source_before + source_after).astype(BF16)
    grad_inputs = (start_here + start_before).astype(BF16)
    grads = finish(
        where,
        shards,
        block,
        columns,
        pieces,
        ((block, 512),) * 8
        + ((block, hidden), (chunks * block, 512))
        + ((1, block),) * TAG_ROW
        + ((tag_table.shape[0], block),),
    )
    return (
        output.reshape(batch, rows, 512),
        grad_inputs,
        grad_encoded,
        *grads[:10],
        *(part.reshape(block) for part in grads[10:-1]),
        grads[-1],
    )


def solution(mesh):
    rows = P("fsdp", "seq", None)
    by_row = P("fsdp", None)
    vector = P("fsdp")
    tags = P(None, "fsdp")
    return jax.shard_map(
        on_device,
        mesh=mesh,
        in_specs=(rows,) * 3 + (by_row,) * 15 + (vector,) * 6 + (tags,),
        out_specs=(rows,) * 3 + (by_row,) * 10 + (vector,) * 6 + (tags,),
        check_vma=False,
    )
```
